32 devices in a mesh: gx: 4 (over y, core), gy: 8 (over z, x).
Axes of the slice: x: 2, y: 2, z: 4, core: 2. Of those that a mesh axis runs over, the one named last changes fastest.
Arguments:
- features: bfloat16 [256, 110592], P('gx', 'gy'), may hold values from -6 to 6
- first_weight: bfloat16 [110592, 768], P(('gy', 'gx')), may hold values from -0.01953125 to 0.01953125
- second_weight: bfloat16 [768, 512], replicated, may hold values from -0.21875 to 0.21875
- centres: bfloat16 [155648, 512], P(('gx', 'gy')), may hold values from -6 to 6
- active: int32 [155648], P(('gx', 'gy')), may hold values from 0 to 16127, as said below
- labels: int32 [256], replicated, may hold values from 0 to 516095, as said below
Outputs:
- loss: float32 [], replicated
- grad_first: bfloat16 [110592, 768], P(('gy', 'gx'))
- grad_second: bfloat16 [768, 512], replicated
- grad_centres: bfloat16 [155648, 512], P(('gx', 'gy'))
The draws below stay inside these ranges and needn't reach their ends.
Inputs may be any that keep to these rules, and one draw needn't show every extreme that they name: Each shard's 4864 entries are distinct and increasing; entry c names class (c // 4864) * 16128 + active[c]. `labels`: every image's class is among the sampled classes, so exactly one centre matches it.
All inputs are finite; a program needn't handle non-finite values.
Results may differ from the reference program's by a relative error of at most 0.0075.
Values may be sent and summed in bfloat16 or wider, within the bound.
No kernel may reach another device: no remote copies, remote signals or barrier semaphores. Data moves between devices by JAX's collectives and lax.ppermute only.
A program may use at most 128 MiB of HBM per device.

```python
import jax
import jax.numpy as jnp
from jax import lax

F = 110592
H = 768
E = 512
CLS_DEV = 16128
CEN_DEV = 4864
B = 256
CENTRES = 155648
NCLASS = 516096
N_GX = 4
N_GY = 8


def choose_classes(key):
    base = jax.random.fold_in(key, 7)
    label_key, order_key = jax.random.split(base)
    shard_count = NCLASS // CLS_DEV
    labels = jax.random.randint(label_key, (B,), 0, NCLASS).astype(jnp.int32)
    labels = labels.at[0].set(0).at[B - 1].set(NCLASS - 1)
    marked = jnp.zeros((NCLASS,), jnp.int32).at[labels].set(1).reshape(shard_count, CLS_DEV)
    local_ids = jnp.arange(CLS_DEV, dtype=jnp.int32)[None, :]
    ends = ((local_ids == 0) | (local_ids == CLS_DEV - 1)).astype(jnp.int32)
    boosted = jnp.maximum(marked, ends)
    scores = jax.random.randint(order_key, (shard_count, CLS_DEV), 0, 16384).astype(jnp.int32) * CLS_DEV + local_ids
    scores = scores + boosted * 2 ** 28
    chosen = lax.top_k(scores, CEN_DEV)[1].astype(jnp.int32)
    chosen = jnp.sort(chosen, axis=1)
    return (labels, chosen.reshape(-1))


def draw_active(key, part):
    return choose_classes(key)[1]


def draw_labels(key, part):
    return choose_classes(key)[0]


def block_levels(stream_key, extent, cuts, low, top_value):
    loudness, own = 1.0, jax.random.fold_in(stream_key, 6)
    for position, shards_of in cuts:
        steps = jnp.exp(jax.random.uniform(jax.random.fold_in(own, position), (shards_of,), jnp.float32, low / len(cuts), top_value / len(cuts)))
        loudness = loudness * jnp.repeat(steps, extent[position] // shards_of).reshape([-1 if axis == position else 1 for axis in range(len(extent))])
    return loudness


def bell_draw(key, dims, width, reach, cuts=(), kind=jnp.bfloat16):
    values = jax.random.normal(key, dims, jnp.float32) * width
    if len(cuts) > 0:
        values = block_levels(key, dims, cuts, -0.22, 0.18) * values
    return jnp.clip(values, min=-reach, max=reach).astype(kind)


def setup_inputs(seed: int = 0) -> dict:
    streams_of = jax.random.split(jax.random.key(seed), 7)
    return {
        "features": bell_draw(streams_of[0], (B, F), 1.0, 6.0, ((0, 4), (1, 8))),
        "first_weight": bell_draw(streams_of[1], (F, H), F ** -0.5, 0.01953125, ((0, 32),)),
        "second_weight": bell_draw(streams_of[2], (H, E), H ** -0.5, 0.21875),
        "centres": bell_draw(streams_of[3], (CENTRES, E), 1.0, 6.0, ((0, 32),)),
        "active": draw_active(jax.random.fold_in(streams_of[6], 71), 0),
        "labels": draw_labels(jax.random.fold_in(streams_of[6], 71), 0),
    }


LOGIT_SCALE = 64.0
COS_MARGIN = 0.4
NORM_EPSILON = 1e-06

def reference(features, first_weight, second_weight, centres, active, labels):
    hidden = jnp.dot(features, first_weight, preferred_element_type=jnp.float32)
    activation, gelu_back = jax.vjp(jax.nn.gelu, hidden)
    act_half = activation.astype(jnp.bfloat16)
    embedding = jnp.dot(act_half, second_weight, preferred_element_type=jnp.float32)
    inv_embed = lax.rsqrt(lax.optimization_barrier(jnp.sum(embedding * embedding, axis=1, keepdims=True)) + NORM_EPSILON)
    unit = embedding * inv_embed
    unit_half = unit.astype(jnp.bfloat16)
    image_count = labels.shape[0]
    shards = N_GX * N_GY
    cen_blocks = centres.reshape(shards, CEN_DEV, centres.shape[1])
    act_blocks = active.reshape(shards, CEN_DEV)
    shard_ids = jnp.arange(shards, dtype=jnp.int32)

    def block_terms(shard, cen_block, act_block):
        cen = cen_block.astype(jnp.float32)
        inv_cen = lax.rsqrt(lax.optimization_barrier(jnp.sum(cen * cen, axis=1, keepdims=True)) + NORM_EPSILON)
        normed = cen * inv_cen
        normed_half = normed.astype(jnp.bfloat16)
        cosine = jnp.dot(unit_half, normed_half.T, preferred_element_type=jnp.float32)
        classes = (shard * CLS_DEV + act_block).astype(jnp.int32)
        positive = (labels[:, None] == classes[None, :]).astype(jnp.float32)
        logits = LOGIT_SCALE * (cosine - COS_MARGIN * positive)
        exp_terms = jnp.exp(logits - LOGIT_SCALE)
        return (inv_cen, normed, normed_half, positive, logits, exp_terms)

    def first_pass(sums, inputs):
        shard, cen_block, act_block = inputs
        parts = block_terms(shard, cen_block, act_block)
        positive, logits, exp_terms = (parts[3], parts[4], parts[5])
        return ((sums[0] + lax.optimization_barrier(jnp.sum(exp_terms, axis=1)), sums[1] + lax.optimization_barrier(jnp.sum(positive * logits, axis=1))), None)
    zeros = jnp.zeros((image_count,), jnp.float32)
    (totals, target), unused = lax.scan(first_pass, (zeros, zeros), (shard_ids, cen_blocks, act_blocks))

    def second_pass(sums, inputs):
        shard, cen_block, act_block = inputs
        inv_cen, normed, normed_half, positive, logits, exp_terms = block_terms(shard, cen_block, act_block)
        weighted = jnp.dot(exp_terms.astype(jnp.bfloat16), normed_half, preferred_element_type=jnp.float32)
        picked = jnp.dot(positive.astype(jnp.bfloat16), normed_half, preferred_element_type=jnp.float32)
        coeff = (LOGIT_SCALE / image_count * (exp_terms / totals[:, None] - positive)).astype(jnp.bfloat16)
        grad_normed = jnp.dot(coeff.T, unit_half, preferred_element_type=jnp.float32)
        grad_cen = inv_cen * (grad_normed - normed * lax.optimization_barrier(jnp.sum(grad_normed * normed, axis=1, keepdims=True)))
        return ((sums[0] + weighted, sums[1] + picked), grad_cen.astype(jnp.bfloat16))
    zero_rows = jnp.zeros((image_count, unit.shape[1]), jnp.float32)
    (weighted, picked), grad_blocks = lax.scan(second_pass, (zero_rows, zero_rows), (shard_ids, cen_blocks, act_blocks))
    grad_centres = grad_blocks.reshape(centres.shape)
    grad_unit = LOGIT_SCALE / image_count * (weighted / totals[:, None] - picked)
    grad_embed = inv_embed * (grad_unit - unit * lax.optimization_barrier(jnp.sum(grad_unit * unit, axis=1, keepdims=True)))
    grad_embed_half = grad_embed.astype(jnp.bfloat16)
    grad_second = jnp.dot(act_half.T, grad_embed_half, preferred_element_type=jnp.float32).astype(jnp.bfloat16)
    grad_act = jnp.dot(grad_embed_half, second_weight.T, preferred_element_type=jnp.float32)
    grad_hidden, = gelu_back(grad_act)
    grad_hidden_half = grad_hidden.astype(jnp.bfloat16)
    grad_first = jnp.dot(features.T, grad_hidden_half, preferred_element_type=jnp.float32).astype(jnp.bfloat16)
    loss = jnp.mean(LOGIT_SCALE + jnp.log(totals) - target)
    return (loss, grad_first, grad_second, grad_centres)
```

```python
import jax
import jax.numpy as jnp
from jax import lax
from jax.sharding import Mesh, PartitionSpec as P

CLS_DEV = 16128


LOGIT_SCALE = 64.0
COS_MARGIN = 0.4
NORM_EPSILON = 1e-06

PIECE_SCALE = 2.0**64

F32, BF16 = jnp.float32, jnp.bfloat16


def core_swap(x):
    return lax.ppermute(x, "core", [(0, 1), (1, 0)])


def pieces(x):
    high = lax.reduce_precision(x, 8, 7)
    rest = x - high
    middle = lax.reduce_precision(rest, 8, 7)
    return [part.astype(BF16) for part in (high, middle, rest - middle)]


def shards(features, first_weight, second_weight, centres, active, labels):
    rows, gy_count = lax.axis_size("row"), lax.axis_size("gy")
    y, core, gy = lax.axis_index("row"), lax.axis_index("core"), lax.axis_index("gy")
    chips = rows * gy_count
    chip = y * gy_count + gy
    device = (y * 2 + core) * gy_count + gy
    image_count = labels.shape[0]
    half = image_count // 2
    group = features.shape[0]
    own = half // chips
    depth = first_weight.shape[0]

    blocks = {}
    for dy in range(rows):
        for dc in range(2):
            if dy == 0 and dc == 0:
                target = y * 2 + core
                blocks[dy, dc] = lax.dynamic_slice_in_dim(features, target * depth, depth, axis=1)
                continue
            target = ((y + dy) % rows) * 2 + (core ^ dc)
            part = lax.dynamic_slice_in_dim(features, target * depth, depth, axis=1)
            perm = [
                (a * 2 + b, ((a + dy) % rows) * 2 + (b ^ dc)) for a in range(rows) for b in range(2)
            ]
            blocks[dy, dc] = lax.ppermute(part, ("row", "core"), perm)
    order = (y - jnp.arange(rows)) % rows
    halves = []
    for dc in range(2):
        stack = jnp.stack([blocks[dy, dc] for dy in range(rows)])
        if rows == 2:
            stack = jnp.where(y == 0, stack, stack[::-1])
        else:
            stack = stack[order]
        halves.append(stack.reshape(half, depth))
    block_rows = jnp.concatenate(halves)

    marks = labels.reshape(rows, 2, group).transpose(1, 0, 2)
    marks = jnp.where(core == 0, marks, marks[::-1]).reshape(image_count)

    cen = centres.astype(F32)
    inv_cen = lax.rsqrt(jnp.sum(cen * cen, axis=1, keepdims=True) + NORM_EPSILON)
    normed = cen * inv_cen
    normed_half = normed.astype(BF16)
    classes = device * CLS_DEV + active
    positive = (marks[:, None] == classes[None, :]).astype(F32)
    picked = jnp.dot(positive.astype(BF16), normed_half, preferred_element_type=F32).astype(BF16)
    picked = picked[:half] + core_swap(picked[half:])
    picked = lax.all_to_all(picked.reshape(chips, own, -1), ("row", "gy"), 0, 0, tiled=True)
    picked = jnp.sum(picked.astype(F32), axis=0)

    part = jnp.dot(block_rows, first_weight, preferred_element_type=F32)
    part = (part[:half] + core_swap(part[half:])).astype(BF16)
    part = lax.all_to_all(part.reshape(chips, own, -1), ("row", "gy"), 0, 0, tiled=True)
    hidden = jnp.sum(part.astype(F32), axis=0).astype(BF16)
    hidden = jnp.broadcast_to(hidden[None], (chips,) + hidden.shape)
    hidden = lax.all_to_all(hidden, ("row", "gy"), 0, 0, tiled=True).reshape(half, -1)
    hidden = jnp.concatenate([hidden, core_swap(hidden)]).astype(F32)

    activation, gelu_back = jax.vjp(jax.nn.gelu, hidden)
    act_half = activation.astype(BF16)
    embedding = jnp.dot(act_half, second_weight, preferred_element_type=F32)
    inv_embed = lax.rsqrt(jnp.sum(embedding * embedding, axis=1, keepdims=True) + NORM_EPSILON)
    unit = embedding * inv_embed
    unit_half = unit.astype(BF16)

    cosine = jnp.dot(unit_half, normed_half.T, preferred_element_type=F32)
    logits = LOGIT_SCALE * (cosine - COS_MARGIN * positive)
    exp_terms = jnp.exp(logits - LOGIT_SCALE)
    row_total = jnp.sum(exp_terms, axis=1)
    row_target = jnp.sum(positive * logits, axis=1)
    weighted = jnp.dot(exp_terms.astype(BF16), normed_half, preferred_element_type=F32)

    weighted = weighted[:half] + core_swap(weighted[half:])
    sums = jnp.stack([row_total * PIECE_SCALE, row_target])
    sums = sums + jnp.roll(core_swap(sums), half, axis=1)
    total_pieces, target_pieces = pieces(sums[0]), pieces(sums[1])
    nothing = jnp.zeros((2 * image_count,), BF16)
    riding = jnp.concatenate(total_pieces + target_pieces + [nothing]).reshape(own, -1)
    riding = jnp.broadcast_to(riding[None], (chips,) + riding.shape)
    width = weighted.shape[1]
    sent = jnp.concatenate([weighted.astype(BF16).reshape(chips, own, width), riding], axis=2)
    sent = lax.all_to_all(sent, ("row", "gy"), 0, 0, tiled=True).astype(F32)
    sent = jnp.sum(sent, axis=0)
    weighted = sent[:, :width]
    sums = sent[:, width:].reshape(-1)[: 6 * image_count].reshape(2, 3, image_count).sum(axis=1)
    totals, target = sums[0] * (1.0 / PIECE_SCALE), sums[1]

    factor = LOGIT_SCALE / image_count
    mine = chip * own
    totals_own = lax.dynamic_slice_in_dim(totals, mine, own)
    unit_own = lax.dynamic_slice_in_dim(unit, mine, own)
    inv_own = lax.dynamic_slice_in_dim(inv_embed, mine, own)
    grad_unit = factor * (weighted / totals_own[:, None] - picked)
    grad_embed = inv_own * (grad_unit - unit_own * jnp.sum(grad_unit * unit_own, axis=1, keepdims=True))
    grad_embed = grad_embed.astype(BF16)
    grad_embed = jnp.broadcast_to(grad_embed[None], (chips,) + grad_embed.shape)
    grad_embed = lax.all_to_all(grad_embed, ("row", "gy"), 0, 0, tiled=True).reshape(half, -1)
    grad_embed = jnp.concatenate([grad_embed, core_swap(grad_embed)])

    coeff = (factor * (exp_terms / totals[:, None] - positive)).astype(BF16)
    grad_normed = jnp.dot(coeff.T, unit_half, preferred_element_type=F32)
    grad_cen = inv_cen * (
        grad_normed - normed * jnp.sum(grad_normed * normed, axis=1, keepdims=True)
    )
    loss = jnp.mean(LOGIT_SCALE + jnp.log(totals) - target)

    grad_second = jnp.dot(act_half.T, grad_embed, preferred_element_type=F32)
    grad_act = jnp.dot(grad_embed, second_weight.T, preferred_element_type=F32)
    (grad_hidden,) = gelu_back(grad_act)
    grad_first = jnp.dot(block_rows.T, grad_hidden.astype(BF16), preferred_element_type=F32)
    return (
        loss,
        grad_first.astype(BF16),
        grad_second.astype(BF16),
        grad_cen.astype(BF16),
    )


def solution(mesh):
    gx_count, gy_count = mesh.shape["gx"], mesh.shape["gy"]
    fine = Mesh(mesh.devices.reshape(gx_count // 2, 2, gy_count), ("row", "core", "gy"))
    gx = ("row", "core")
    placed = (
        P(gx, "gy"),
        P(("gy",) + gx, None),
        P(),
        P(gx + ("gy",), None),
        P(gx + ("gy",)),
        P(),
    )
    return jax.shard_map(
        shards,
        mesh=fine,
        in_specs=placed,
        out_specs=(P(), P(("gy",) + gx, None), P(), P(gx + ("gy",), None)),
        check_vma=False,
    )
```

```python
import functools

import jax
import jax.numpy as jnp
from jax import lax
from jax.experimental import pallas as pl
from jax.experimental.pallas import tpu as pltpu
from jax.sharding import Mesh, PartitionSpec as P

CLS_DEV = 16128


LOGIT_SCALE = 64.0
COS_MARGIN = 0.4
NORM_EPSILON = 1e-06

PIECE_SCALE = 2.0**64

F32, BF16 = jnp.float32, jnp.bfloat16
MIB = 2**20
VMEM = pl.BlockSpec(memory_space=pltpu.VMEM)
ANY = pl.BlockSpec(memory_space=pl.ANY)

NN = (((1,), (0,)), ((), ()))
NT = (((1,), (1,)), ((), ()))


def dot(a, b, dims=NN):
    return lax.dot_general(a, b, dims, preferred_element_type=F32)


def tile_of(extent, most, unit=16):
    return max(t for t in range(unit, most + 1, unit) if extent % t == 0)


def gelu_parts(v):
    scale = 0.7978845608028654
    cube = 0.044715
    square = v * v
    bend = jnp.tanh(scale * (v + cube * square * v))
    left = 0.5 * (1.0 + bend)
    slope = left + 0.5 * v * (1.0 - bend * bend) * scale * (1.0 + 3.0 * cube * square)
    return v * left, slope


def prep_kernel(cen_ref, marks_ref, classes_ref, half_ref, picked_ref, total):
    step = pl.program_id(0)
    cen = cen_ref[...].astype(F32)
    inv = lax.rsqrt(jnp.sum(cen * cen, axis=1, keepdims=True) + NORM_EPSILON)
    half = (cen * inv).astype(BF16)
    half_ref[...] = half
    match = (marks_ref[...] == classes_ref[0]).astype(F32).astype(BF16)
    found = dot(match, half)

    @pl.when(step == 0)
    def _():
        total[...] = found

    @pl.when(step > 0)
    def _():
        total[...] += found

    @pl.when(step == pl.num_programs(0) - 1)
    def _():
        picked_ref[...] = total[...].astype(BF16)


def prep(centres, marks, classes):
    count, width = centres.shape
    images = marks.shape[0]
    tile = tile_of(count, 1280)
    steps = count // tile
    return pl.pallas_call(
        prep_kernel,
        grid=(steps,),
        in_specs=[
            pl.BlockSpec((tile, width), lambda i: (i, 0)),
            pl.BlockSpec((images, 1), lambda i: (0, 0)),
            pl.BlockSpec((1, 1, tile), lambda i: (i, 0, 0)),
        ],
        out_specs=[
            pl.BlockSpec((tile, width), lambda i: (i, 0)),
            pl.BlockSpec((images, width), lambda i: (0, 0)),
        ],
        out_shape=[
            jax.ShapeDtypeStruct((count, width), BF16),
            jax.ShapeDtypeStruct((images, width), BF16),
        ],
        scratch_shapes=[pltpu.VMEM((images, width), F32)],
        compiler_params=pltpu.CompilerParams(vmem_limit_bytes=32 * MIB),
        cost_estimate=pl.CostEstimate(
            flops=2 * count * width * images, bytes_accessed=4 * count * width, transcendentals=0
        ),
    )(centres, marks, classes.reshape(steps, 1, tile))


def softmax_kernel(
    tile,
    hid_a,
    hid_b,
    second,
    marks,
    classes,
    half_hbm,
    keep,
    send,
    sums,
    unit_out,
    half,
    unit,
    weighted,
    total,
    target,
    cos_even,
    cos_odd,
    sem,
):
    steps = classes.shape[0]

    def copy(i):
        rows = pl.ds(pl.multiple_of(i * tile, tile), tile)
        return pltpu.make_async_copy(half_hbm.at[rows], half.at[rows], sem.at[i])

    def start(i, carry):
        copy(i).start()
        return carry

    lax.fori_loop(0, steps, start, 0)

    group = hid_a.shape[0]
    for place, hid in enumerate((hid_a, hid_b)):
        act, _ = gelu_parts(hid[...].astype(F32))
        embedding = dot(act.astype(BF16), second[...])
        inv = lax.rsqrt(jnp.sum(embedding * embedding, axis=1, keepdims=True) + NORM_EPSILON)
        unit[pl.ds(place * group, group), :] = (embedding * inv).astype(BF16)
    unit_out[...] = unit[...]
    weighted[...] = jnp.zeros_like(weighted)
    total[...] = jnp.zeros_like(total)
    target[...] = jnp.zeros_like(target)

    def part(i):
        return half[pl.ds(pl.multiple_of(i * tile, tile), tile), :]

    def cosine(i, ref):
        copy(i).wait()
        ref[...] = dot(unit[...], part(i), NT)

    def fold(x):
        return functools.reduce(jnp.add, [x[:, c : c + 128] for c in range(0, tile, 128)])

    def process(i, ref):
        positive = marks[...] == classes[i]
        logits = LOGIT_SCALE * (ref[...] - jnp.where(positive, COS_MARGIN, 0.0))
        exp_terms = jnp.exp(logits - LOGIT_SCALE)
        total[...] += fold(exp_terms)
        target[...] += fold(jnp.where(positive, logits, 0.0))
        weighted[...] += dot(exp_terms.astype(BF16), part(i))

    cosine(0, cos_even)

    def pair(j, carry):
        cosine(2 * j + 1, cos_odd)
        process(2 * j, cos_even)
        cosine(2 * j + 2, cos_even)
        process(2 * j + 1, cos_odd)
        return carry

    lax.fori_loop(0, (steps - 1) // 2, pair, 0)
    if steps % 2:
        process(steps - 1, cos_even)
    else:
        cosine(steps - 1, cos_odd)
        process(steps - 2, cos_even)
        process(steps - 1, cos_odd)

    keep[...] = weighted[:group]
    send[...] = weighted[group:]
    sums[...] = jnp.zeros_like(sums)
    sums[0:1, :] = jnp.sum(total[...].T, axis=0, keepdims=True)
    sums[1:2, :] = jnp.sum(target[...].T, axis=0, keepdims=True)


def softmax_sums(hid_a, hid_b, second, marks, classes, half):
    count, width = half.shape
    group = hid_a.shape[0]
    images = marks.shape[0]
    tile = tile_of(count, 256, 128)
    steps = count // tile
    return pl.pallas_call(
        functools.partial(softmax_kernel, tile),
        in_specs=[VMEM] * 5 + [ANY],
        out_specs=[VMEM] * 4,
        out_shape=[
            jax.ShapeDtypeStruct((group, width), F32),
            jax.ShapeDtypeStruct((group, width), F32),
            jax.ShapeDtypeStruct((8, images), F32),
            jax.ShapeDtypeStruct((images, width), BF16),
        ],
        scratch_shapes=[
            pltpu.VMEM((count, width), BF16),
            pltpu.VMEM((images, width), BF16),
            pltpu.VMEM((images, width), F32),
            pltpu.VMEM((images, 128), F32),
            pltpu.VMEM((images, 128), F32),
            pltpu.VMEM((images, tile), F32),
            pltpu.VMEM((images, tile), F32),
            pltpu.SemaphoreType.DMA((steps,)),
        ],
        compiler_params=pltpu.CompilerParams(vmem_limit_bytes=40 * MIB),
        cost_estimate=pl.CostEstimate(
            flops=4 * count * width * images, bytes_accessed=4 * count * width, transcendentals=0
        ),
    )(hid_a, hid_b, second, marks, classes.reshape(steps, 1, tile), half)


def centres_kernel(factor, cen_ref, classes_ref, marks_ref, unit_ref, inv_total_ref, out_ref):
    cen = cen_ref[...].astype(F32)
    inv = lax.rsqrt(jnp.sum(cen * cen, axis=1, keepdims=True) + NORM_EPSILON)
    normed = cen * inv
    unit = unit_ref[...]
    cosine = dot(normed.astype(BF16), unit, NT)
    positive = classes_ref[...] == marks_ref[...]
    logits = LOGIT_SCALE * (cosine - jnp.where(positive, COS_MARGIN, 0.0))
    exp_terms = jnp.exp(logits - LOGIT_SCALE)
    coeff = factor * (exp_terms * inv_total_ref[...] - jnp.where(positive, 1.0, 0.0))
    grad = dot(coeff.astype(BF16), unit)
    grad = inv * (grad - normed * jnp.sum(grad * normed, axis=1, keepdims=True))
    out_ref[...] = grad.astype(BF16)


def grad_centres(centres, classes, marks, unit, inv_total):
    count, width = centres.shape
    images = unit.shape[0]
    tile = tile_of(count, 1280 if images <= 256 else 256)
    return pl.pallas_call(
        functools.partial(centres_kernel, LOGIT_SCALE / images),
        grid=(count // tile,),
        in_specs=[
            pl.BlockSpec((tile, width), lambda i: (i, 0)),
            pl.BlockSpec((tile, 1), lambda i: (i, 0)),
            pl.BlockSpec((1, images), lambda i: (0, 0)),
            pl.BlockSpec((images, width), lambda i: (0, 0)),
            pl.BlockSpec((1, images), lambda i: (0, 0)),
        ],
        out_specs=pl.BlockSpec((tile, width), lambda i: (i, 0)),
        out_shape=jax.ShapeDtypeStruct((count, width), BF16),
        compiler_params=pltpu.CompilerParams(vmem_limit_bytes=40 * MIB),
        cost_estimate=pl.CostEstimate(
            flops=4 * count * width * images, bytes_accessed=4 * count * width, transcendentals=0
        ),
    )(centres, classes, marks, unit, inv_total)


def turn_kernel(rows, place_ref, *refs):
    blocks, out_ref, stack = refs[:-2], refs[-2], refs[-1]
    group, depth = blocks[0].shape
    y = place_ref[0]
    for i, block in enumerate(blocks):
        dy, dc = divmod(i, 2)
        where = dc * rows + lax.rem(y - dy + rows, rows)
        stack[pl.ds(pl.multiple_of(where * group, group), group), :] = block[...]
    width = tile_of(depth, 128)

    if width == 128:

        def turn(i, carry):
            columns = pl.ds(pl.multiple_of(i * width, width), width)
            out_ref[columns, :] = stack[:, columns].T
            return carry

        lax.fori_loop(0, depth // width, turn, 0)
    else:
        out_ref[...] = stack[...].T


def turned(rows, place, blocks):
    group, depth = blocks[0].shape
    images = group * len(blocks)
    return pl.pallas_call(
        functools.partial(turn_kernel, rows),
        in_specs=[pl.BlockSpec(memory_space=pltpu.SMEM)] + [VMEM] * len(blocks),
        out_specs=VMEM,
        out_shape=jax.ShapeDtypeStruct((depth, images), BF16),
        scratch_shapes=[pltpu.VMEM((images, depth), BF16)],
        compiler_params=pltpu.CompilerParams(vmem_limit_bytes=16 * MIB),
        cost_estimate=pl.CostEstimate(
            flops=0, bytes_accessed=4 * depth * images, transcendentals=0
        ),
    )(place, *blocks)


def tail_kernel(grad_a, grad_b, second, slope, act, turned_ref, first_ref, second_ref, grad_hidden):
    group = grad_a.shape[0]

    @pl.when(pl.program_id(0) == 0)
    def _():
        for place, grad in enumerate((grad_a, grad_b)):
            rows = pl.ds(place * group, group)
            grad_act = dot(grad[...], second[...], NT)
            grad_hidden[rows, :] = (grad_act * slope[rows, :]).astype(BF16)
        second_ref[...] = (dot(act[:, :group], grad_a[...]) + dot(act[:, group:], grad_b[...])).astype(BF16)

    first_ref[...] = dot(turned_ref[...], grad_hidden[...]).astype(BF16)


def tail(grad_a, grad_b, second, slope, act, turned_features):
    depth, images = turned_features.shape
    hidden, width = second.shape
    group = grad_a.shape[0]
    tile = tile_of(depth, 512)

    def whole(*shape):
        return pl.BlockSpec(shape, lambda i: (0,) * len(shape))

    return pl.pallas_call(
        tail_kernel,
        grid=(depth // tile,),
        in_specs=[
            whole(group, width),
            whole(group, width),
            whole(hidden, width),
            whole(images, hidden),
            whole(hidden, images),
            pl.BlockSpec((tile, images), lambda i: (i, 0)),
        ],
        out_specs=[pl.BlockSpec((tile, hidden), lambda i: (i, 0)), whole(hidden, width)],
        out_shape=[
            jax.ShapeDtypeStruct((depth, hidden), BF16),
            jax.ShapeDtypeStruct((hidden, width), BF16),
        ],
        scratch_shapes=[pltpu.VMEM((images, hidden), BF16)],
        compiler_params=pltpu.CompilerParams(vmem_limit_bytes=40 * MIB),
        cost_estimate=pl.CostEstimate(
            flops=2 * depth * hidden * images, bytes_accessed=2 * depth * (hidden + images), transcendentals=0
        ),
    )(grad_a, grad_b, second, slope, act, turned_features)


def core_swap(x):
    return lax.ppermute(x, "core", [(0, 1), (1, 0)])


def to_chips(x):
    return lax.all_to_all(x, ("row", "gy"), 0, 0, tiled=True)


def to_all_chips(x, chips):
    x = to_chips(jnp.broadcast_to(x[None], (chips,) + x.shape))
    return x.reshape(-1, x.shape[-1])


def shards(features, first_weight, second_weight, centres, active, labels):
    rows, gy_count = lax.axis_size("row"), lax.axis_size("gy")
    y, core, gy = lax.axis_index("row"), lax.axis_index("core"), lax.axis_index("gy")
    chips = rows * gy_count
    chip = y * gy_count + gy
    device = (y * 2 + core) * gy_count + gy
    image_count = labels.shape[0]
    half = image_count // 2
    group = features.shape[0]
    own = half // chips
    depth = first_weight.shape[0]

    blocks = {}
    source = features
    for dc in (1, 0):
        for dy in list(range(1, rows)) + [0]:
            target = ((y + dy) % rows) * 2 + (core ^ dc)
            part = lax.dynamic_slice_in_dim(source, target * depth, depth, axis=1)
            if (dy, dc) == (0, 0):
                blocks[dy, dc] = part
                continue
            perm = [
                (a * 2 + b, ((a + dy) % rows) * 2 + (b ^ dc)) for a in range(rows) for b in range(2)
            ]
            blocks[dy, dc] = lax.ppermute(part, ("row", "core"), perm)

    marks = labels.reshape(rows, 2, group).transpose(1, 0, 2)
    marks = jnp.where(core == 0, marks, marks[::-1]).reshape(image_count)
    marks_row, marks_column = marks[None, :], marks[:, None]
    classes = device * CLS_DEV + active

    normed_half, picked = prep(centres, marks_column, classes)
    picked = picked[:half] + core_swap(picked[half:])
    picked = to_chips(picked.reshape(chips, own, -1))
    picked = jnp.sum(picked.astype(F32), axis=0)

    def partial_hidden(*names):
        return jnp.dot(
            jnp.concatenate([blocks[n] for n in names]), first_weight, preferred_element_type=F32
        )

    others = list(range(1, rows))
    near = partial_hidden((0, 1), (0, 0))
    far_send = partial_hidden(*[(dy, 1) for dy in others])
    near_keep = near[group:] + core_swap(near[:group])
    far_got = core_swap(far_send)
    far_keep = partial_hidden(*[(dy, 0) for dy in others]) + far_got
    if rows == 2:
        part = jnp.where(
            y == 0,
            jnp.concatenate([near_keep, far_keep]),
            jnp.concatenate([far_keep, near_keep]),
        )
    else:
        part = jnp.concatenate([near_keep, far_keep]).reshape(rows, group, -1)
        part = part[(y - jnp.arange(rows)) % rows]
    part = to_chips(part.astype(BF16).reshape(chips, own, -1))
    hidden_own = jnp.sum(part.astype(F32), axis=0).astype(BF16)
    hid_a = to_all_chips(hidden_own, chips)
    hid_b = core_swap(hid_a)

    embed_own = jnp.dot(
        gelu_parts(hidden_own.astype(F32))[0].astype(BF16), second_weight, preferred_element_type=F32
    )
    inv_own = lax.rsqrt(jnp.sum(embed_own * embed_own, axis=1, keepdims=True) + NORM_EPSILON)
    unit_own = embed_own * inv_own

    weighted, weighted_send, sums, unit_half = softmax_sums(
        hid_a, hid_b, second_weight, marks_column, classes, normed_half
    )
    act, slope = gelu_parts(jnp.concatenate([hid_a, hid_b]).astype(F32))
    act_turned = act.astype(BF16).T

    weighted = weighted + core_swap(weighted_send)
    sums = sums[:2]
    sums = sums + jnp.roll(core_swap(sums), half, axis=1)
    sums = sums * jnp.array([[PIECE_SCALE], [1.0]], F32)
    high = lax.reduce_precision(sums, 8, 7)
    rest = sums - high
    middle = lax.reduce_precision(rest, 8, 7)
    riding = jnp.concatenate([high, middle, rest - middle, jnp.zeros_like(sums)]).astype(BF16)
    riding = riding.reshape(own, -1)
    riding = jnp.broadcast_to(riding[None], (chips,) + riding.shape)
    width = weighted.shape[1]
    sent = jnp.concatenate([weighted.astype(BF16).reshape(chips, own, width), riding], axis=2)
    sent = jnp.sum(to_chips(sent).astype(F32), axis=0)
    weighted = sent[:, :width]
    sums = sent[:, width:].reshape(4, 2, image_count).sum(axis=0)
    totals, target = sums[0:1] * (1.0 / PIECE_SCALE), sums[1:2]

    factor = LOGIT_SCALE / image_count
    totals_own = lax.dynamic_slice_in_dim(totals, chip * own, own, axis=1).reshape(own, 1)
    grad_unit = factor * (weighted / totals_own - picked)
    grad_embed = inv_own * (grad_unit - unit_own * jnp.sum(grad_unit * unit_own, axis=1, keepdims=True))
    grad_a = to_all_chips(grad_embed.astype(BF16), chips)
    grad_b = core_swap(grad_a)

    grad_cen = grad_centres(centres, classes[:, None], marks_row, unit_half, 1.0 / totals)
    loss = jnp.mean(LOGIT_SCALE + jnp.log(totals) - target)

    place = jnp.reshape(y, (1,)).astype(jnp.int32)
    order = [(dy, dc) for dy in range(rows) for dc in range(2)]
    turned_features = turned(rows, place, [blocks[n] for n in order])
    grad_first, grad_second = tail(
        grad_a, grad_b, second_weight, slope, act_turned, turned_features
    )
    return loss, grad_first, grad_second, grad_cen


def solution(mesh):
    gx_count, gy_count = mesh.shape["gx"], mesh.shape["gy"]
    fine = Mesh(mesh.devices.reshape(gx_count // 2, 2, gy_count), ("row", "core", "gy"))
    gx = ("row", "core")
    placed = (
        P(gx, "gy"),
        P(("gy",) + gx, None),
        P(),
        P(gx + ("gy",), None),
        P(gx + ("gy",)),
        P(),
    )
    return jax.shard_map(
        shards,
        mesh=fine,
        in_specs=placed,
        out_specs=(P(), P(("gy",) + gx, None), P(), P(gx + ("gy",), None)),
        check_vma=False,
    )
```

```python
import functools

import jax
import jax.numpy as jnp
from jax import lax
from jax.experimental import pallas as pl
from jax.experimental.pallas import tpu as pltpu
from jax.sharding import Mesh, PartitionSpec as P

CLS_DEV = 16128


LOGIT_SCALE = 64.0
COS_MARGIN = 0.4
NORM_EPSILON = 1e-06

PIECE_SCALE = 2.0**64

F32, BF16 = jnp.float32, jnp.bfloat16
MIB = 2**20
VMEM = pl.BlockSpec(memory_space=pltpu.VMEM)
HBM = pl.BlockSpec(memory_space=pltpu.HBM)

NN = (((1,), (0,)), ((), ()))
NT = (((1,), (1,)), ((), ()))


def dot(a, b, dims=NN):
    return lax.dot_general(a, b, dims, preferred_element_type=F32)


def tile_of(extent, most, unit=16):
    return max(t for t in range(unit, most + 1, unit) if extent % t == 0)


def gelu_parts(v):
    scale = 0.7978845608028654
    cube = 0.044715
    square = v * v
    bend = jnp.tanh(scale * (v + cube * square * v))
    left = 0.5 * (1.0 + bend)
    slope = left + 0.5 * v * (1.0 - bend * bend) * scale * (1.0 + 3.0 * cube * square)
    return v * left, slope


def row_to_column(row):
    return jnp.broadcast_to(row, (8, row.shape[1])).T[:, :1]


def each(count, plain, step):
    if plain:
        for i in range(count):
            step(i)
    else:

        def run(i, carry):
            step(i)
            return carry

        lax.fori_loop(0, count, run, 0)


def rows_at(i, tile):
    return pl.ds(i * tile if isinstance(i, int) else pl.multiple_of(i * tile, tile), tile)


def params(mib):
    return pltpu.CompilerParams(vmem_limit_bytes=mib * MIB)


def cost(flops, moved):
    return pl.CostEstimate(flops=flops, bytes_accessed=moved, transcendentals=0)


def prep_kernel(plain, marks, classes, cen_hbm, half_hbm, picked, cen, half, total, in_sem, out_sem):
    steps, tile = classes.shape
    column = row_to_column(marks[...])

    def load(i):
        rows = rows_at(i, tile)
        return pltpu.make_async_copy(cen_hbm.at[rows], cen.at[rows], in_sem.at[i])

    def store(i):
        rows = rows_at(i, tile)
        return pltpu.make_async_copy(half.at[rows], half_hbm.at[rows], out_sem.at[i])

    each(steps, plain, lambda i: load(i).start())
    total[...] = jnp.zeros_like(total)

    def step(i):
        load(i).wait()
        rows = rows_at(i, tile)
        block = cen[rows, :].astype(F32)
        inv = lax.rsqrt(jnp.sum(block * block, axis=1, keepdims=True) + NORM_EPSILON)
        block = (block * inv).astype(BF16)
        half[rows, :] = block
        store(i).start()
        match = jnp.where(column == classes[pl.ds(i, 1), :], 1.0, 0.0).astype(BF16)
        total[...] += dot(match, block)

    each(steps, plain, step)
    picked[...] = total[...].astype(BF16)
    each(steps, plain, lambda i: store(i).wait())


def prep(centres, marks, classes):
    count, width = centres.shape
    images = marks.shape[1]
    steps = classes.shape[0]
    return pl.pallas_call(
        functools.partial(prep_kernel, images <= 256),
        in_specs=[VMEM, VMEM, HBM],
        out_specs=[HBM, VMEM],
        out_shape=[
            jax.ShapeDtypeStruct((count, width), BF16),
            jax.ShapeDtypeStruct((images, width), BF16),
        ],
        scratch_shapes=[
            pltpu.VMEM((count, width), BF16),
            pltpu.VMEM((count, width), BF16),
            pltpu.VMEM((images, width), F32),
            pltpu.SemaphoreType.DMA((steps,)),
            pltpu.SemaphoreType.DMA((steps,)),
        ],
        compiler_params=params(28),
        cost_estimate=cost(2 * count * width * images, 8 * count * width),
    )(marks, classes, centres)


def softmax_kernel(
    plain,
    hid_a_hbm,
    hid_b_hbm,
    second_hbm,
    marks,
    classes,
    half_hbm,
    keep,
    send,
    sums,
    unit_hbm,
    hid_a,
    hid_b,
    second,
    half,
    unit,
    weighted,
    first_sem,
    in_sem,
    out_sem,
):
    steps, tile = classes.shape
    firsts = [
        pltpu.make_async_copy(source, place, first_sem.at[i])
        for i, (source, place) in enumerate(
            ((hid_a_hbm, hid_a), (second_hbm, second), (hid_b_hbm, hid_b))
        )
    ]
    for copy in firsts:
        copy.start()

    def load(i):
        rows = rows_at(i, tile)
        return pltpu.make_async_copy(half_hbm.at[rows], half.at[rows], in_sem.at[i])

    each(steps, plain, lambda i: load(i).start())

    group = hid_a.shape[0]
    images = 2 * group
    column = row_to_column(marks[...])
    firsts[0].wait()
    firsts[1].wait()
    for place, hid in enumerate((hid_a, hid_b)):
        if place == 1:
            firsts[2].wait()
        act, _ = gelu_parts(hid[...].astype(F32))
        embedding = dot(act.astype(BF16), second[...])
        inv = lax.rsqrt(jnp.sum(embedding * embedding, axis=1, keepdims=True) + NORM_EPSILON)
        unit[pl.ds(place * group, group), :] = (embedding * inv).astype(BF16)
    store = pltpu.make_async_copy(unit, unit_hbm, out_sem)
    store.start()
    weighted[...] = jnp.zeros_like(weighted)

    def step(i, sums):
        load(i).wait()
        block = half[rows_at(i, tile), :]
        cosine = dot(unit[...], block, NT)
        positive = column == classes[pl.ds(i, 1), :]
        logits = LOGIT_SCALE * (cosine - jnp.where(positive, COS_MARGIN, 0.0))
        exp_terms = jnp.exp(logits - LOGIT_SCALE)
        weighted[...] += dot(exp_terms.astype(BF16), block)
        total = jnp.sum(exp_terms, axis=1, keepdims=True)
        target = jnp.sum(jnp.where(positive, logits, 0.0), axis=1, keepdims=True)
        return sums[0] + total, sums[1] + target

    total = target = jnp.zeros((images, 1), F32)
    if plain:
        for i in range(steps):
            total, target = step(i, (total, target))
    else:
        total, target = lax.fori_loop(0, steps, step, (total, target))
    keep[...] = weighted[:group]
    send[...] = weighted[group:]
    for i, column in enumerate((total, target)):
        sums[i : i + 1, :] = jnp.broadcast_to(column, (images, 128)).T[:1]
    store.wait()


def softmax_sums(hid_a, hid_b, second, marks, classes, half):
    count, width = half.shape
    group = hid_a.shape[0]
    images = marks.shape[1]
    steps = classes.shape[0]
    return pl.pallas_call(
        functools.partial(softmax_kernel, images <= 256),
        in_specs=[HBM] * 3 + [VMEM] * 2 + [HBM],
        out_specs=[VMEM] * 3 + [HBM],
        out_shape=[
            jax.ShapeDtypeStruct((group, width), F32),
            jax.ShapeDtypeStruct((group, width), F32),
            jax.ShapeDtypeStruct((2, images), F32),
            jax.ShapeDtypeStruct((images, width), BF16),
        ],
        scratch_shapes=[
            pltpu.VMEM(hid_a.shape, BF16),
            pltpu.VMEM(hid_b.shape, BF16),
            pltpu.VMEM(second.shape, BF16),
            pltpu.VMEM((count, width), BF16),
            pltpu.VMEM((images, width), BF16),
            pltpu.VMEM((images, width), F32),
            pltpu.SemaphoreType.DMA((3,)),
            pltpu.SemaphoreType.DMA((steps,)),
            pltpu.SemaphoreType.DMA,
        ],
        compiler_params=params(57),
        cost_estimate=cost(4 * count * width * images, 4 * count * width),
    )(hid_a, hid_b, second, marks, classes, half)


def centres_kernel(
    plain, factor, marks, classes, inv_total, unit_ref, cen_hbm, out_hbm, cen, out, in_sem, out_sem
):
    steps, tile = classes.shape
    columns = jnp.concatenate([classes[...], jnp.zeros((-steps % 8, tile), jnp.int32)]).T

    def load(i):
        rows = rows_at(i, tile)
        return pltpu.make_async_copy(cen_hbm.at[rows], cen.at[rows], in_sem.at[i])

    def store(i):
        rows = rows_at(i, tile)
        return pltpu.make_async_copy(out.at[rows], out_hbm.at[rows], out_sem.at[i])

    each(steps, True, lambda i: load(i).start())
    unit = unit_ref[...]

    def step(i):
        load(i).wait()
        rows = rows_at(i, tile)
        block = cen[rows, :].astype(F32)
        inv = lax.rsqrt(jnp.sum(block * block, axis=1, keepdims=True) + NORM_EPSILON)
        normed = block * inv
        cosine = dot(normed.astype(BF16), unit, NT)
        positive = columns[:, i : i + 1] == marks[...]
        logits = LOGIT_SCALE * (cosine - jnp.where(positive, COS_MARGIN, 0.0))
        exp_terms = jnp.exp(logits - LOGIT_SCALE)
        coeff = factor * (exp_terms * inv_total[...] - jnp.where(positive, 1.0, 0.0))
        grad = dot(coeff.astype(BF16), unit)
        grad = inv * (grad - normed * jnp.sum(grad * normed, axis=1, keepdims=True))
        out[rows, :] = grad.astype(BF16)
        store(i).start()

    each(steps, True, step)
    each(steps, True, lambda i: store(i).wait())


def grad_centres(centres, classes, marks, unit, inv_total):
    count, width = centres.shape
    images = unit.shape[0]
    steps = classes.shape[0]
    return pl.pallas_call(
        functools.partial(centres_kernel, images <= 256, LOGIT_SCALE / images),
        in_specs=[VMEM] * 4 + [HBM],
        out_specs=HBM,
        out_shape=jax.ShapeDtypeStruct((count, width), BF16),
        scratch_shapes=[
            pltpu.VMEM((count, width), BF16),
            pltpu.VMEM((count, width), BF16),
            pltpu.SemaphoreType.DMA((steps,)),
            pltpu.SemaphoreType.DMA((steps,)),
        ],
        compiler_params=params(57),
        cost_estimate=cost(4 * count * width * images, 8 * count * width),
    )(marks, classes, inv_total, unit, centres)


def turn_kernel(rows, place_ref, *refs):
    blocks, out_ref, stack = refs[:-2], refs[-2], refs[-1]
    group, depth = blocks[0].shape
    y = place_ref[0]
    for i, block in enumerate(blocks):
        dy, dc = divmod(i, 2)
        where = dc * rows + lax.rem(y - dy + rows, rows)
        stack[pl.ds(pl.multiple_of(where * group, group), group), :] = block[...]
    width = tile_of(depth, 128)

    if width == 128:

        def turn(i, carry):
            columns = pl.ds(pl.multiple_of(i * width, width), width)
            out_ref[columns, :] = stack[:, columns].T
            return carry

        lax.fori_loop(0, depth // width, turn, 0)
    else:
        out_ref[...] = stack[...].T


def turned(rows, place, blocks):
    group, depth = blocks[0].shape
    images = group * len(blocks)
    return pl.pallas_call(
        functools.partial(turn_kernel, rows),
        in_specs=[pl.BlockSpec(memory_space=pltpu.SMEM)] + [VMEM] * len(blocks),
        out_specs=VMEM,
        out_shape=jax.ShapeDtypeStruct((depth, images), BF16),
        scratch_shapes=[pltpu.VMEM((images, depth), BF16)],
        compiler_params=params(16),
        cost_estimate=cost(0, 4 * depth * images),
    )(place, *blocks)


def tail_kernel(
    grad_a,
    grad_b,
    hid_a,
    hid_b,
    second,
    turned_hbm,
    first_hbm,
    second_out,
    features,
    out,
    grad_hidden,
    in_sem,
    out_sem,
):
    group = grad_a.shape[0]
    steps = in_sem.shape[0]
    tile = out.shape[0] // steps

    def load(i):
        rows = rows_at(i, tile)
        return pltpu.make_async_copy(turned_hbm.at[rows], features.at[rows], in_sem.at[i])

    def store(i):
        rows = rows_at(i, tile)
        return pltpu.make_async_copy(out.at[rows], first_hbm.at[rows], out_sem.at[i])

    each(steps, True, lambda i: load(i).start())
    acts = []
    for place, (grad, hid) in enumerate(((grad_a, hid_a), (grad_b, hid_b))):
        act, slope = gelu_parts(hid[...].astype(F32))
        acts.append(act.astype(BF16))
        grad_act = dot(grad[...], second[...], NT)
        grad_hidden[pl.ds(place * group, group), :] = (grad_act * slope).astype(BF16)

    def step(i):
        load(i).wait()
        rows = rows_at(i, tile)
        out[rows, :] = dot(features[rows, :], grad_hidden[...]).astype(BF16)
        store(i).start()

    each(steps, True, step)
    act = jnp.concatenate(acts)
    grad = jnp.concatenate([grad_a[...], grad_b[...]])
    second_out[...] = dot(act.T, grad).astype(BF16)
    each(steps, True, lambda i: store(i).wait())


def tail(grad_a, grad_b, hid_a, hid_b, second, turned_features):
    depth, images = turned_features.shape
    hidden, width = second.shape
    steps = depth // tile_of(depth, 1200)
    return pl.pallas_call(
        tail_kernel,
        in_specs=[VMEM] * 5 + [HBM],
        out_specs=[HBM, VMEM],
        out_shape=[
            jax.ShapeDtypeStruct((depth, hidden), BF16),
            jax.ShapeDtypeStruct((hidden, width), BF16),
        ],
        scratch_shapes=[
            pltpu.VMEM((depth, images), BF16),
            pltpu.VMEM((depth, hidden), BF16),
            pltpu.VMEM((images, hidden), BF16),
            pltpu.SemaphoreType.DMA((steps,)),
            pltpu.SemaphoreType.DMA((steps,)),
        ],
        compiler_params=params(57),
        cost_estimate=cost(2 * depth * hidden * images, 2 * depth * (hidden + images)),
    )(grad_a, grad_b, hid_a, hid_b, second, turned_features)


def core_swap(x):
    return lax.ppermute(x, "core", [(0, 1), (1, 0)])


def to_chips(x):
    return lax.all_to_all(x, ("row", "gy"), 0, 0, tiled=True)


def to_all_chips(x, chips):
    x = to_chips(jnp.broadcast_to(x[None], (chips,) + x.shape))
    return x.reshape(-1, x.shape[-1])


def shards(features, first_weight, second_weight, centres, active, labels):
    rows, gy_count = lax.axis_size("row"), lax.axis_size("gy")
    y, core, gy = lax.axis_index("row"), lax.axis_index("core"), lax.axis_index("gy")
    chips = rows * gy_count
    chip = y * gy_count + gy
    device = (y * 2 + core) * gy_count + gy
    image_count = labels.shape[0]
    half = image_count // 2
    group = features.shape[0]
    own = half // chips
    depth = first_weight.shape[0]

    blocks = {}
    source = features
    for dc in (1, 0):
        for dy in list(range(1, rows)) + [0]:
            target = ((y + dy) % rows) * 2 + (core ^ dc)
            part = lax.dynamic_slice_in_dim(source, target * depth, depth, axis=1)
            if (dy, dc) == (0, 0):
                blocks[dy, dc] = part
                continue
            perm = [
                (a * 2 + b, ((a + dy) % rows) * 2 + (b ^ dc)) for a in range(rows) for b in range(2)
            ]
            blocks[dy, dc] = lax.ppermute(part, ("row", "core"), perm)

    marks = labels.reshape(rows, 2, group).transpose(1, 0, 2)
    marks = jnp.where(core == 0, marks, marks[::-1]).reshape(image_count)
    marks = marks[None, :]
    count = active.shape[0]
    tile = tile_of(count, 1280 if image_count <= 256 else 256)
    classes = (device * CLS_DEV + active).reshape(count // tile, tile)

    first_arrived, marks, classes = lax.optimization_barrier((blocks[0, 1], marks, classes))
    blocks[0, 1] = first_arrived
    normed_half, picked = prep(centres, marks, classes)
    picked = picked[:half] + core_swap(picked[half:])

    def partial_hidden(*names):
        return jnp.dot(
            jnp.concatenate([blocks[n] for n in names]), first_weight, preferred_element_type=F32
        )

    others = list(range(1, rows))
    near = partial_hidden((0, 1), (0, 0))
    far_send = partial_hidden(*[(dy, 1) for dy in others])
    near_keep = near[group:] + core_swap(near[:group])
    far_got = core_swap(far_send)
    last = [blocks[dy, 0] for dy in others]
    last, normed_half, picked = lax.optimization_barrier((last, normed_half, picked))
    for dy, block in zip(others, last):
        blocks[dy, 0] = block
    far_keep = partial_hidden(*[(dy, 0) for dy in others]) + far_got
    if rows == 2:
        part = jnp.where(
            y == 0,
            jnp.concatenate([near_keep, far_keep]),
            jnp.concatenate([far_keep, near_keep]),
        )
    else:
        part = jnp.concatenate([near_keep, far_keep]).reshape(rows, group, -1)
        part = part[(y - jnp.arange(rows)) % rows].reshape(half, -1)
    wide = part.shape[1]
    part = jnp.concatenate([part.astype(BF16), picked], axis=1)
    part = to_chips(part.reshape(chips, own, -1))
    place = jnp.reshape(y, (1,)).astype(jnp.int32)
    order = [(dy, dc) for dy in range(rows) for dc in range(2)]
    turned_features = turned(rows, place, [blocks[n] for n in order])
    part, turned_features = lax.optimization_barrier((part, turned_features))
    part = jnp.sum(part.astype(F32), axis=0)
    hidden_own, picked = part[:, :wide].astype(BF16), part[:, wide:]
    hid_a = to_all_chips(hidden_own, chips)
    hid_b = core_swap(hid_a)

    embed_own = jnp.dot(
        gelu_parts(hidden_own.astype(F32))[0].astype(BF16), second_weight, preferred_element_type=F32
    )
    inv_own = lax.rsqrt(jnp.sum(embed_own * embed_own, axis=1, keepdims=True) + NORM_EPSILON)
    unit_own = embed_own * inv_own

    weighted, weighted_send, sums, unit_half = softmax_sums(
        hid_a, hid_b, second_weight, marks, classes, normed_half
    )
    weighted = weighted + core_swap(weighted_send)
    sums = sums + jnp.roll(core_swap(sums), half, axis=1)
    sums = sums * jnp.array([[PIECE_SCALE], [1.0]], F32)
    high = lax.reduce_precision(sums, 8, 7)
    rest = sums - high
    middle = lax.reduce_precision(rest, 8, 7)
    riding = jnp.concatenate([high, middle, rest - middle, jnp.zeros_like(sums)]).astype(BF16)
    riding = riding.reshape(own, -1)
    riding = jnp.broadcast_to(riding[None], (chips,) + riding.shape)
    width = weighted.shape[1]
    sent = jnp.concatenate([weighted.astype(BF16).reshape(chips, own, width), riding], axis=2)
    sent = jnp.sum(to_chips(sent).astype(F32), axis=0)
    weighted = sent[:, :width]
    sums = sent[:, width:].reshape(4, 2, image_count).sum(axis=0)
    totals, target = sums[0:1] * (1.0 / PIECE_SCALE), sums[1:2]

    factor = LOGIT_SCALE / image_count
    totals_own = lax.dynamic_slice_in_dim(totals, chip * own, own, axis=1).reshape(own, 1)
    grad_unit = factor * (weighted / totals_own - picked)
    grad_embed = inv_own * (grad_unit - unit_own * jnp.sum(grad_unit * unit_own, axis=1, keepdims=True))
    grad_cen = grad_centres(centres, classes, marks, unit_half, 1.0 / totals)
    grad_a = to_all_chips(grad_embed.astype(BF16), chips)
    grad_a, grad_cen = lax.optimization_barrier((grad_a, grad_cen))
    grad_b = core_swap(grad_a)
    loss = jnp.mean(LOGIT_SCALE + jnp.log(totals) - target)
    grad_first, grad_second = tail(grad_a, grad_b, hid_a, hid_b, second_weight, turned_features)
    return loss, grad_first, grad_second, grad_cen


def solution(mesh):
    gx_count, gy_count = mesh.shape["gx"], mesh.shape["gy"]
    fine = Mesh(mesh.devices.reshape(gx_count // 2, 2, gy_count), ("row", "core", "gy"))
    gx = ("row", "core")
    placed = (
        P(gx, "gy"),
        P(("gy",) + gx, None),
        P(),
        P(gx + ("gy",), None),
        P(gx + ("gy",)),
        P(),
    )
    return jax.shard_map(
        shards,
        mesh=fine,
        in_specs=placed,
        out_specs=(P(), P(("gy",) + gx, None), P(), P(gx + ("gy",), None)),
        check_vma=False,
    )
```

```python
import functools

import jax
import jax.numpy as jnp
from jax import lax
from jax.experimental import pallas as pl
from jax.experimental.pallas import tpu as pltpu
from jax.sharding import Mesh, PartitionSpec as P

CLS_DEV = 16128


LOGIT_SCALE = 64.0
COS_MARGIN = 0.4
NORM_EPSILON = 1e-06

POWER = LOGIT_SCALE * 1.4426950408889634

PIECE_SCALE = 2.0**64

SMALLEST = 1.1754944e-38

AHEAD = 2

F32, BF16 = jnp.float32, jnp.bfloat16
MIB = 2**20
VMEM = pl.BlockSpec(memory_space=pltpu.VMEM)
HBM = pl.BlockSpec(memory_space=pltpu.HBM)

NN = (((1,), (0,)), ((), ()))
NT = (((1,), (1,)), ((), ()))


def dot(a, b, dims=NN):
    return lax.dot_general(a, b, dims, preferred_element_type=F32)


def tile_of(extent, most, unit=16):
    return max(t for t in range(unit, most + 1, unit) if extent % t == 0)


def gelu_parts(v):
    scale = 0.7978845608028654
    cube = 0.044715
    square = v * v
    bend = jnp.tanh(scale * (v + cube * square * v))
    left = 0.5 * (1.0 + bend)
    slope = left + 0.5 * v * (1.0 - bend * bend) * scale * (1.0 + 3.0 * cube * square)
    return v * left, slope


def row_to_column(row):
    return jnp.broadcast_to(row, (8, row.shape[1])).T[:, :1]


def each(count, plain, step):
    if plain:
        for i in range(count):
            step(i)
    else:

        def run(i, carry):
            step(i)
            return carry

        lax.fori_loop(0, count, run, 0)


def rows_at(i, tile):
    return pl.ds(i * tile if isinstance(i, int) else pl.multiple_of(i * tile, tile), tile)


def params(mib):
    return pltpu.CompilerParams(vmem_limit_bytes=mib * MIB)


def cost(flops, moved):
    return pl.CostEstimate(flops=flops, bytes_accessed=moved, transcendentals=0)


def exp_terms_of(cosine, positive):
    return jnp.exp2(
        cosine * POWER - jnp.where(positive, POWER * (1.0 + COS_MARGIN), POWER)
    )


def prep_kernel(plain, marks, classes, cen_hbm, half_hbm, picked, cen, half, total, in_sem, out_sem):
    steps, tile = classes.shape
    column = row_to_column(marks[...])

    def load(i):
        rows = rows_at(i, tile)
        return pltpu.make_async_copy(cen_hbm.at[rows], cen.at[rows], in_sem.at[i])

    def store(i):
        rows = rows_at(i, tile)
        return pltpu.make_async_copy(half.at[rows], half_hbm.at[rows], out_sem.at[i])

    each(steps, plain, lambda i: load(i).start())
    total[...] = jnp.zeros_like(total)

    def step(i):
        load(i).wait()
        rows = rows_at(i, tile)
        block = cen[rows, :].astype(F32)
        inv = lax.rsqrt(jnp.sum(block * block, axis=1, keepdims=True) + NORM_EPSILON)
        block = (block * inv).astype(BF16)
        half[rows, :] = block
        store(i).start()
        match = jnp.where(column == classes[pl.ds(i, 1), :], 1.0, 0.0).astype(BF16)
        total[...] += dot(match, block)

    each(steps, plain, step)
    picked[...] = total[...].astype(BF16)
    each(steps, plain, lambda i: store(i).wait())


def prep(centres, marks, classes):
    count, width = centres.shape
    images = marks.shape[1]
    steps = classes.shape[0]
    return pl.pallas_call(
        functools.partial(prep_kernel, images <= 256),
        in_specs=[VMEM, VMEM, HBM],
        out_specs=[HBM, VMEM],
        out_shape=[
            jax.ShapeDtypeStruct((5 * count, width), BF16),
            jax.ShapeDtypeStruct((images, width), BF16),
        ],
        scratch_shapes=[
            pltpu.VMEM((count, width), BF16),
            pltpu.VMEM((count, width), BF16),
            pltpu.VMEM((images, width), F32),
            pltpu.SemaphoreType.DMA((steps,)),
            pltpu.SemaphoreType.DMA((steps,)),
        ],
        compiler_params=params(28),
        cost_estimate=cost(2 * count * width * images, 8 * count * width),
    )(marks, classes, centres)


def softmax_kernel(
    plain,
    hid_a_hbm,
    hid_b_hbm,
    second_hbm,
    marks,
    classes,
    half_hbm,
    keep,
    send,
    shared,
    hid_a,
    hid_b,
    second,
    half,
    unit,
    weighted,
    first_sem,
    in_sem,
    out_sem,
):
    steps, tile = classes.shape
    firsts = [
        pltpu.make_async_copy(source, place, first_sem.at[i])
        for i, (source, place) in enumerate(
            ((hid_a_hbm, hid_a), (second_hbm, second), (hid_b_hbm, hid_b))
        )
    ]
    for copy in firsts:
        copy.start()

    def load(i):
        rows = rows_at(i, tile)
        return pltpu.make_async_copy(half_hbm.at[rows], half.at[rows], in_sem.at[i])

    load(0).start()
    group = hid_a.shape[0]
    images = 2 * group
    column = row_to_column(marks[...])
    firsts[0].wait()
    firsts[1].wait()
    each(steps - 1, plain, lambda i: load(i + 1).start())
    for place, hid in enumerate((hid_a, hid_b)):
        if place == 1:
            firsts[2].wait()
        act, _ = gelu_parts(hid[...].astype(F32))
        embedding = dot(act.astype(BF16), second[...])
        inv = lax.rsqrt(jnp.sum(embedding * embedding, axis=1, keepdims=True) + NORM_EPSILON)
        unit[pl.ds(place * group, group), :] = (embedding * inv).astype(BF16)
    store = pltpu.make_async_copy(unit, shared.at[pl.ds(steps * tile, images)], out_sem)
    store.start()
    weighted[...] = jnp.zeros_like(weighted)

    def step(i, sums):
        load(i).wait()
        block = half[rows_at(i, tile), :]
        cosine = dot(unit[...], block, NT)
        positive = column == classes[pl.ds(i, 1), :]
        exp_terms = exp_terms_of(cosine, positive)
        weighted[...] += dot(exp_terms.astype(BF16), block)
        total = jnp.sum(exp_terms, axis=1, keepdims=True)
        target = jnp.sum(jnp.where(positive, cosine - COS_MARGIN, 0.0), axis=1, keepdims=True)
        return sums[0] + total, sums[1] + target

    total = target = jnp.zeros((images, 1), F32)
    if plain:
        for i in range(steps):
            total, target = step(i, (total, target))
    else:
        total, target = lax.fori_loop(0, steps, step, (total, target))
    sums = [jnp.broadcast_to(x, (images, 128)).T[:1] for x in (total, LOGIT_SCALE * target)]
    width = keep.shape[1]
    rows = [x[:, c : c + width] for x in sums for c in range(0, images, width)]
    rows = [jnp.pad(x, ((0, 0), (0, width - x.shape[1]))) for x in rows]
    rows = jnp.concatenate(rows + [jnp.zeros((8 - len(rows), width), F32)])
    for ref, part in ((keep, weighted[:group]), (send, weighted[group:])):
        ref[:group, :] = part
        ref[group:, :] = rows
    store.wait()


def softmax_sums(hid_a, hid_b, second, marks, classes, half):
    width = half.shape[1]
    group = hid_a.shape[0]
    images = marks.shape[1]
    steps = classes.shape[0]
    count = classes.size
    return pl.pallas_call(
        functools.partial(softmax_kernel, images <= 256),
        in_specs=[HBM] * 3 + [VMEM] * 2 + [HBM],
        out_specs=[VMEM] * 2 + [HBM],
        input_output_aliases={5: 2},
        out_shape=[
            jax.ShapeDtypeStruct((group + 8, width), F32),
            jax.ShapeDtypeStruct((group + 8, width), F32),
            jax.ShapeDtypeStruct(half.shape, BF16),
        ],
        scratch_shapes=[
            pltpu.VMEM(hid_a.shape, BF16),
            pltpu.VMEM(hid_b.shape, BF16),
            pltpu.VMEM(second.shape, BF16),
            pltpu.VMEM((count, width), BF16),
            pltpu.VMEM((images, width), BF16),
            pltpu.VMEM((images, width), F32),
            pltpu.SemaphoreType.DMA((3,)),
            pltpu.SemaphoreType.DMA((steps,)),
            pltpu.SemaphoreType.DMA,
        ],
        compiler_params=params(40),
        cost_estimate=cost(4 * count * width * images, 4 * count * width),
    )(hid_a, hid_b, second, marks, classes, half)


def chunked(steps, tile, pairs, sem):
    def copies(i):
        rows = rows_at(i, tile)
        return [
            pltpu.make_async_copy(source.at[rows], target.at[rows], sem.at[p, i])
            for p, (source, target) in enumerate(pairs)
        ]

    def start(i):
        for copy in copies(i):
            copy.start()

    def wait(i):
        for copy in copies(i):
            copy.wait()

    return start, wait


def columns_of(classes):
    pad = jnp.zeros((-classes.shape[0] % 8, classes.shape[1]), jnp.int32)
    return jnp.concatenate([classes[...], pad]).T


def inverse_norm(block):
    return lax.rsqrt(jnp.sum(block * block, axis=1, keepdims=True) + NORM_EPSILON)


def terms_kernel(marks, classes, cen_hbm, shared_hbm, out_hbm, cen, unit, out, unit_sem, in_sem, out_sem):
    steps, tile = classes.shape
    count = steps * tile
    unit_copy = pltpu.make_async_copy(shared_hbm.at[pl.ds(count, unit.shape[0])], unit, unit_sem)
    unit_copy.start()
    load, loaded = chunked(steps, tile, [(cen_hbm, cen)], in_sem)
    store, stored = chunked(steps, tile, [(out, out_hbm)], out_sem)
    for i in range(min(AHEAD, steps)):
        load(i)
    columns = columns_of(classes)
    unit_copy.wait()
    for i in range(steps):
        loaded(i)
        if i + AHEAD < steps:
            load(i + AHEAD)
        rows = rows_at(i, tile)
        block = cen[rows, :].astype(F32)
        cosine = dot((block * inverse_norm(block)).astype(BF16), unit[...], NT)
        positive = columns[:, i : i + 1] == marks[...]
        terms = exp_terms_of(cosine, positive)
        out[rows, :] = jnp.where(positive, -jnp.maximum(terms, SMALLEST), terms)
        store(i)
    for i in range(steps):
        stored(i)


def turned_terms(centres, classes, marks, shared):
    count, width = centres.shape
    images = marks.shape[1]
    steps = classes.shape[0]
    return pl.pallas_call(
        terms_kernel,
        in_specs=[VMEM] * 2 + [HBM] * 2,
        out_specs=HBM,
        out_shape=jax.ShapeDtypeStruct((count, images), F32),
        scratch_shapes=[
            pltpu.VMEM((count, width), BF16),
            pltpu.VMEM((images, width), BF16),
            pltpu.VMEM((count, images), F32),
            pltpu.SemaphoreType.DMA,
            pltpu.SemaphoreType.DMA((1, steps)),
            pltpu.SemaphoreType.DMA((1, steps)),
        ],
        compiler_params=params(57),
        cost_estimate=cost(2 * count * width * images, 8 * count * width),
    )(marks, classes, centres, shared)


def centres_kernel(
    factor,
    totals_hbm,
    cen_hbm,
    shared_hbm,
    terms_hbm,
    out_hbm,
    totals,
    unit,
    cen,
    terms,
    out,
    first_sem,
    in_sem,
    out_sem,
):
    steps = in_sem.shape[1]
    count = cen.shape[0]
    tile = count // steps
    firsts = [
        pltpu.make_async_copy(totals_hbm, totals, first_sem.at[0]),
        pltpu.make_async_copy(shared_hbm.at[pl.ds(count, unit.shape[0])], unit, first_sem.at[1]),
    ]
    load, loaded = chunked(steps, tile, [(cen_hbm, cen), (terms_hbm, terms)], in_sem)
    store, stored = chunked(steps, tile, [(out, out_hbm)], out_sem)
    for copy in firsts:
        copy.start()
    for i in range(min(AHEAD + 1, steps)):
        load(i)
    for copy in firsts:
        copy.wait()
    share = factor / totals[...]
    for i in range(steps):
        loaded(i)
        if i + AHEAD + 1 < steps:
            load(i + AHEAD + 1)
        rows = rows_at(i, tile)
        block = cen[rows, :].astype(F32)
        inv = inverse_norm(block)
        signed = terms[rows, :]
        coeff = jnp.abs(signed) * share - jnp.where(signed < 0.0, factor, 0.0)
        grad = dot(coeff.astype(BF16), unit[...])
        along = jnp.sum(grad * block, axis=1, keepdims=True) * (inv * inv)
        out[rows, :] = (inv * (grad - block * along)).astype(BF16)
        store(i)
    for i in range(steps):
        stored(i)


def grad_centres(centres, terms, shared, totals):
    count, width = centres.shape
    images = terms.shape[1]
    steps = count // tile_of(count, 640)
    return pl.pallas_call(
        functools.partial(centres_kernel, LOGIT_SCALE / images),
        in_specs=[HBM] * 4,
        out_specs=HBM,
        out_shape=jax.ShapeDtypeStruct((count, width), BF16),
        scratch_shapes=[
            pltpu.VMEM((1, images), F32),
            pltpu.VMEM((images, width), BF16),
            pltpu.VMEM((count, width), BF16),
            pltpu.VMEM((count, images), F32),
            pltpu.VMEM((count, width), BF16),
            pltpu.SemaphoreType.DMA((2,)),
            pltpu.SemaphoreType.DMA((2, steps)),
            pltpu.SemaphoreType.DMA((1, steps)),
        ],
        compiler_params=params(57),
        cost_estimate=cost(4 * count * width * images, 8 * count * width),
    )(totals, centres, shared, terms)


def turn_kernel(rows, place_ref, *refs):
    blocks, out_ref, stack = refs[:-2], refs[-2], refs[-1]
    group, depth = blocks[0].shape
    y = place_ref[0]
    for i, block in enumerate(blocks):
        dy, dc = divmod(i, 2)
        where = dc * rows + lax.rem(y - dy + rows, rows)
        stack[pl.ds(pl.multiple_of(where * group, group), group), :] = block[...]
    width = tile_of(depth, 128)

    if width == 128:

        def turn(i, carry):
            columns = pl.ds(pl.multiple_of(i * width, width), width)
            out_ref[columns, :] = stack[:, columns].T
            return carry

        lax.fori_loop(0, depth // width, turn, 0)
    else:
        out_ref[...] = stack[...].T


def turned(rows, place, blocks):
    group, depth = blocks[0].shape
    images = group * len(blocks)
    return pl.pallas_call(
        functools.partial(turn_kernel, rows),
        in_specs=[pl.BlockSpec(memory_space=pltpu.SMEM)] + [VMEM] * len(blocks),
        out_specs=VMEM,
        out_shape=jax.ShapeDtypeStruct((depth, images), BF16),
        scratch_shapes=[pltpu.VMEM((images, depth), BF16)],
        compiler_params=params(57),
        cost_estimate=cost(0, 4 * depth * images),
    )(place, *blocks)


def tail_kernel(
    grad_a,
    grad_b,
    hid_a,
    hid_b,
    second,
    turned_hbm,
    first_hbm,
    second_out,
    features,
    out,
    grad_hidden,
    in_sem,
    out_sem,
):
    group = grad_a.shape[0]
    steps = in_sem.shape[0]
    tile = out.shape[0] // steps

    def load(i):
        rows = rows_at(i, tile)
        return pltpu.make_async_copy(turned_hbm.at[rows], features.at[rows], in_sem.at[i])

    def store(i):
        rows = rows_at(i, tile)
        return pltpu.make_async_copy(out.at[rows], first_hbm.at[rows], out_sem.at[i])

    each(steps, True, lambda i: load(i).start())
    acts = []
    for place, (grad, hid) in enumerate(((grad_a, hid_a), (grad_b, hid_b))):
        act, slope = gelu_parts(hid[...].astype(F32))
        acts.append(act.astype(BF16))
        grad_act = dot(grad[...], second[...], NT)
        grad_hidden[pl.ds(place * group, group), :] = (grad_act * slope).astype(BF16)

    def step(i):
        load(i).wait()
        rows = rows_at(i, tile)
        out[rows, :] = dot(features[rows, :], grad_hidden[...]).astype(BF16)
        store(i).start()

    each(steps, True, step)
    act = jnp.concatenate(acts)
    grad = jnp.concatenate([grad_a[...], grad_b[...]])
    second_out[...] = dot(act.T, grad).astype(BF16)
    each(steps, True, lambda i: store(i).wait())


def tail(grad_a, grad_b, hid_a, hid_b, second, turned_features):
    depth, images = turned_features.shape
    hidden, width = second.shape
    steps = depth // tile_of(depth, 1200)
    return pl.pallas_call(
        tail_kernel,
        in_specs=[VMEM] * 5 + [HBM],
        out_specs=[HBM, VMEM],
        out_shape=[
            jax.ShapeDtypeStruct((depth, hidden), BF16),
            jax.ShapeDtypeStruct((hidden, width), BF16),
        ],
        scratch_shapes=[
            pltpu.VMEM((depth, images), BF16),
            pltpu.VMEM((depth, hidden), BF16),
            pltpu.VMEM((images, hidden), BF16),
            pltpu.SemaphoreType.DMA((steps,)),
            pltpu.SemaphoreType.DMA((steps,)),
        ],
        compiler_params=params(40),
        cost_estimate=cost(2 * depth * hidden * images, 2 * depth * (hidden + images)),
    )(grad_a, grad_b, hid_a, hid_b, second, turned_features)


def assemble_kernel(images, keep, got, out):
    width = keep.shape[1]
    half = keep.shape[0] - 8
    each = -(-images // width)

    def sums(ref):
        lines = [
            jnp.concatenate([ref[half + each * q + r : half + each * q + r + 1, :] for r in range(each)], axis=1)
            for q in range(2)
        ]
        return jnp.concatenate(lines)[:, :images]

    other = sums(got)
    both = sums(keep) + jnp.concatenate([other[:, images // 2 :], other[:, : images // 2]], axis=1)
    scale = jnp.where(lax.broadcasted_iota(jnp.int32, both.shape, 0) == 0, PIECE_SCALE, 1.0)
    both = both * scale
    parts = []
    for _ in range(3):
        part = both.astype(BF16).astype(F32)
        parts.append(part)
        both = both - part
    riding = jnp.concatenate(parts + [jnp.zeros_like(both)])
    out[:, :width] = (keep[:half, :] + got[:half, :]).astype(BF16)
    out[:, width:] = jnp.concatenate([riding] * (half // 8)).astype(BF16)


def assemble(images, keep, got):
    half, width = keep.shape[0] - 8, keep.shape[1]
    return pl.pallas_call(
        functools.partial(assemble_kernel, images),
        in_specs=[VMEM] * 2,
        out_specs=VMEM,
        out_shape=jax.ShapeDtypeStruct((half, width + images), BF16),
        compiler_params=params(16),
        cost_estimate=cost(0, 8 * half * (width + images)),
    )(keep, got)


def core_swap(x):
    return lax.ppermute(x, "core", [(0, 1), (1, 0)])


def to_chips(x):
    return lax.all_to_all(x, ("row", "gy"), 0, 0, tiled=True)


def to_all_chips(x, chips):
    x = to_chips(jnp.broadcast_to(x[None], (chips,) + x.shape))
    return x.reshape(-1, x.shape[-1])


def shards(features, first_weight, second_weight, centres, active, labels):
    rows, gy_count = lax.axis_size("row"), lax.axis_size("gy")
    y, core, gy = lax.axis_index("row"), lax.axis_index("core"), lax.axis_index("gy")
    chips = rows * gy_count
    chip = y * gy_count + gy
    device = (y * 2 + core) * gy_count + gy
    image_count = labels.shape[0]
    half = image_count // 2
    group = features.shape[0]
    own = half // chips
    depth = first_weight.shape[0]

    blocks = {}
    others = list(range(1, rows))
    for dy, dc in [(dy, 1) for dy in others] + [(0, 1)] + [(dy, 0) for dy in others] + [(0, 0)]:
        target = ((y + dy) % rows) * 2 + (core ^ dc)
        if (dy, dc) == (0, 0):
            source, labels = lax.optimization_barrier((features, labels))
            blocks[dy, dc] = lax.dynamic_slice_in_dim(source, target * depth, depth, axis=1)
            continue
        part = lax.dynamic_slice_in_dim(features, target * depth, depth, axis=1)
        perm = [
            (a * 2 + b, ((a + dy) % rows) * 2 + (b ^ dc)) for a in range(rows) for b in range(2)
        ]
        blocks[dy, dc] = lax.ppermute(part, ("row", "core"), perm)

    marks = labels.reshape(rows, 2, group).transpose(1, 0, 2)
    marks = jnp.where(core == 0, marks, marks[::-1]).reshape(image_count)
    marks = marks[None, :]
    count = active.shape[0]
    tile = tile_of(count, 1280 if image_count <= 256 else 256)
    classes = (device * CLS_DEV + active).reshape(count // tile, tile)

    first_arrived, marks, classes = lax.optimization_barrier((blocks[0, 1], marks, classes))
    blocks[0, 1] = first_arrived
    normed_half, picked = prep(centres, marks, classes)
    picked = picked[:half] + core_swap(picked[half:])

    def partial_hidden(*names):
        return jnp.dot(
            jnp.concatenate([blocks[n] for n in names]), first_weight, preferred_element_type=F32
        )

    near = partial_hidden((0, 1), (0, 0))
    early = [blocks[dy, 1] for dy in others]
    early, near, normed_half, picked = lax.optimization_barrier((early, near, normed_half, picked))
    for dy, block in zip(others, early):
        blocks[dy, 1] = block
    far_send = partial_hidden(*[(dy, 1) for dy in others])
    near_keep = near[group:] + core_swap(near[:group])
    far_got = core_swap(far_send)
    last = [blocks[dy, 0] for dy in others]
    last, far_got, near_keep, picked = lax.optimization_barrier((last, far_got, near_keep, picked))
    for dy, block in zip(others, last):
        blocks[dy, 0] = block
    far_keep = partial_hidden(*[(dy, 0) for dy in others]) + far_got
    if rows == 2:
        part = jnp.where(
            y == 0,
            jnp.concatenate([near_keep, far_keep]),
            jnp.concatenate([far_keep, near_keep]),
        )
    else:
        part = jnp.concatenate([near_keep, far_keep]).reshape(rows, group, -1)
        part = part[(y - jnp.arange(rows)) % rows].reshape(half, -1)
    wide = part.shape[1]
    part = jnp.concatenate([part.astype(BF16), picked], axis=1)
    part = to_chips(part.reshape(chips, own, -1))
    place = jnp.reshape(y, (1,)).astype(jnp.int32)
    order = [(dy, dc) for dy in range(rows) for dc in range(2)]
    turned_features = turned(rows, place, [blocks[n] for n in order])
    part, turned_features = lax.optimization_barrier((part, turned_features))
    part = jnp.sum(part.astype(F32), axis=0)
    hidden_own, picked = part[:, :wide].astype(BF16), part[:, wide:]
    hid_a = to_all_chips(hidden_own, chips)
    hid_b = core_swap(hid_a)

    embed_own = jnp.dot(
        gelu_parts(hidden_own.astype(F32))[0].astype(BF16), second_weight, preferred_element_type=F32
    )
    inv_own = lax.rsqrt(jnp.sum(embed_own * embed_own, axis=1, keepdims=True) + NORM_EPSILON)
    unit_own = embed_own * inv_own

    weighted, weighted_send, shared = softmax_sums(
        hid_a, hid_b, second_weight, marks, classes, normed_half
    )
    width = weighted.shape[1]
    sent = assemble(image_count, weighted, core_swap(weighted_send))
    sent, shared = lax.optimization_barrier((sent, shared))
    terms = turned_terms(centres, classes, marks, shared)
    sent, terms = lax.optimization_barrier((to_chips(sent.reshape(chips, own, -1)), terms))
    sent = jnp.sum(sent.astype(F32), axis=0)
    weighted = sent[:, :width]
    sums = sent[:, width:].reshape(4, 2, image_count).sum(axis=0)
    totals, target = sums[0:1] * (1.0 / PIECE_SCALE), sums[1:2]

    factor = LOGIT_SCALE / image_count
    totals_own = lax.dynamic_slice_in_dim(totals, chip * own, own, axis=1).reshape(own, 1)
    grad_unit = factor * (weighted / totals_own - picked)
    grad_embed = inv_own * (grad_unit - unit_own * jnp.sum(grad_unit * unit_own, axis=1, keepdims=True))
    grad_embed = grad_embed.astype(BF16)
    grad_embed = jnp.broadcast_to(grad_embed[None], (chips,) + grad_embed.shape)
    grad_embed, totals, target = lax.optimization_barrier((grad_embed, totals, target))
    grad_cen = grad_centres(centres, terms, shared, totals)
    grad_a = to_chips(grad_embed).reshape(half, -1)
    grad_a, grad_cen = lax.optimization_barrier((grad_a, grad_cen))
    grad_b = core_swap(grad_a)
    loss = jnp.mean(LOGIT_SCALE + jnp.log(totals) - target)
    grad_first, grad_second = tail(grad_a, grad_b, hid_a, hid_b, second_weight, turned_features)
    return loss, grad_first, grad_second, grad_cen


def solution(mesh):
    gx_count, gy_count = mesh.shape["gx"], mesh.shape["gy"]
    fine = Mesh(mesh.devices.reshape(gx_count // 2, 2, gy_count), ("row", "core", "gy"))
    gx = ("row", "core")
    placed = (
        P(gx, "gy"),
        P(("gy",) + gx, None),
        P(),
        P(gx + ("gy",), None),
        P(gx + ("gy",)),
        P(),
    )
    return jax.shard_map(
        shards,
        mesh=fine,
        in_specs=placed,
        out_specs=(P(), P(("gy",) + gx, None), P(), P(gx + ("gy",), None)),
        check_vma=False,
    )
```

```python
import functools

import jax
import jax.numpy as jnp
from jax import lax
from jax.experimental import pallas as pl
from jax.experimental.pallas import tpu as pltpu
from jax.sharding import Mesh, PartitionSpec as P

CLS_DEV = 16128


LOGIT_SCALE = 64.0
COS_MARGIN = 0.4
NORM_EPSILON = 1e-06

POWER = LOGIT_SCALE * 1.4426950408889634

PIECE_SCALE = 2.0**64

SMALLEST = 1.1754944e-38

AHEAD = 2

F32, BF16 = jnp.float32, jnp.bfloat16
MIB = 2**20
VMEM = pl.BlockSpec(memory_space=pltpu.VMEM)
HBM = pl.BlockSpec(memory_space=pltpu.HBM)

NN = (((1,), (0,)), ((), ()))
NT = (((1,), (1,)), ((), ()))


def dot(a, b, dims=NN):
    return lax.dot_general(a, b, dims, preferred_element_type=F32)


def tile_of(extent, most, unit=16):
    return max(t for t in range(unit, most + 1, unit) if extent % t == 0)


def gelu_parts(v):
    scale = 0.7978845608028654
    cube = 0.044715
    square = v * v
    bend = jnp.tanh(scale * (v + cube * square * v))
    left = 0.5 * (1.0 + bend)
    slope = left + 0.5 * v * (1.0 - bend * bend) * scale * (1.0 + 3.0 * cube * square)
    return v * left, slope


def row_to_column(row):
    return jnp.broadcast_to(row, (8, row.shape[1])).T[:, :1]


def each(count, plain, step):
    if plain:
        for i in range(count):
            step(i)
    else:

        def run(i, carry):
            step(i)
            return carry

        lax.fori_loop(0, count, run, 0)


def rows_at(i, tile):
    return pl.ds(i * tile if isinstance(i, int) else pl.multiple_of(i * tile, tile), tile)


def params(mib):
    return pltpu.CompilerParams(vmem_limit_bytes=mib * MIB)


def cost(flops, moved):
    return pl.CostEstimate(flops=flops, bytes_accessed=moved, transcendentals=0)


def exp_terms_of(cosine, positive):
    return jnp.exp2(
        cosine * POWER - jnp.where(positive, POWER * (1.0 + COS_MARGIN), POWER)
    )


def prep_kernel(plain, marks, classes, cen_hbm, half_hbm, picked, cen, half, total, in_sem, out_sem):
    steps, tile = classes.shape
    column = row_to_column(marks[...])

    def load(i):
        rows = rows_at(i, tile)
        return pltpu.make_async_copy(cen_hbm.at[rows], cen.at[rows], in_sem.at[i])

    def store(i):
        rows = rows_at(i, tile)
        return pltpu.make_async_copy(half.at[rows], half_hbm.at[rows], out_sem.at[i])

    each(steps, plain, lambda i: load(i).start())
    total[...] = jnp.zeros_like(total)

    def step(i):
        load(i).wait()
        rows = rows_at(i, tile)
        block = cen[rows, :].astype(F32)
        inv = lax.rsqrt(jnp.sum(block * block, axis=1, keepdims=True) + NORM_EPSILON)
        block = (block * inv).astype(BF16)
        half[rows, :] = block
        store(i).start()
        match = jnp.where(column == classes[pl.ds(i, 1), :], 1.0, 0.0).astype(BF16)
        total[...] += dot(match, block)

    each(steps, plain, step)
    picked[...] = total[...].astype(BF16)
    each(steps, plain, lambda i: store(i).wait())


def prep(centres, marks, classes):
    count, width = centres.shape
    images = marks.shape[1]
    steps = classes.shape[0]
    return pl.pallas_call(
        functools.partial(prep_kernel, images <= 256),
        in_specs=[VMEM, VMEM, HBM],
        out_specs=[HBM, VMEM],
        out_shape=[
            jax.ShapeDtypeStruct((5 * count, width), BF16),
            jax.ShapeDtypeStruct((images, width), BF16),
        ],
        scratch_shapes=[
            pltpu.VMEM((count, width), BF16),
            pltpu.VMEM((count, width), BF16),
            pltpu.VMEM((images, width), F32),
            pltpu.SemaphoreType.DMA((steps,)),
            pltpu.SemaphoreType.DMA((steps,)),
        ],
        compiler_params=params(28),
        cost_estimate=cost(2 * count * width * images, 8 * count * width),
    )(marks, classes, centres)


def softmax_kernel(
    plain,
    hid_a_hbm,
    hid_b_hbm,
    second_hbm,
    marks,
    classes,
    half_hbm,
    keep,
    send,
    shared,
    hid_a,
    hid_b,
    second,
    half,
    unit,
    weighted,
    first_sem,
    in_sem,
    out_sem,
):
    steps, tile = classes.shape
    firsts = [
        pltpu.make_async_copy(source, place, first_sem.at[i])
        for i, (source, place) in enumerate(
            ((hid_a_hbm, hid_a), (second_hbm, second), (hid_b_hbm, hid_b))
        )
    ]
    for copy in firsts:
        copy.start()

    def load(i):
        rows = rows_at(i, tile)
        return pltpu.make_async_copy(half_hbm.at[rows], half.at[rows], in_sem.at[i])

    load(0).start()
    group = hid_a.shape[0]
    images = 2 * group
    column = row_to_column(marks[...])
    firsts[0].wait()
    firsts[1].wait()
    each(steps - 1, plain, lambda i: load(i + 1).start())
    for place, hid in enumerate((hid_a, hid_b)):
        if place == 1:
            firsts[2].wait()
        act, _ = gelu_parts(hid[...].astype(F32))
        embedding = dot(act.astype(BF16), second[...])
        inv = lax.rsqrt(jnp.sum(embedding * embedding, axis=1, keepdims=True) + NORM_EPSILON)
        unit[pl.ds(place * group, group), :] = (embedding * inv).astype(BF16)
    store = pltpu.make_async_copy(unit, shared.at[pl.ds(steps * tile, images)], out_sem)
    store.start()
    weighted[...] = jnp.zeros_like(weighted)

    def step(i, sums):
        load(i).wait()
        block = half[rows_at(i, tile), :]
        cosine = dot(unit[...], block, NT)
        positive = column == classes[pl.ds(i, 1), :]
        exp_terms = exp_terms_of(cosine, positive)
        weighted[...] += dot(exp_terms.astype(BF16), block)
        total = jnp.sum(exp_terms, axis=1, keepdims=True)
        target = jnp.sum(jnp.where(positive, cosine - COS_MARGIN, 0.0), axis=1, keepdims=True)
        return sums[0] + total, sums[1] + target

    total = target = jnp.zeros((images, 1), F32)
    if plain:
        for i in range(steps):
            total, target = step(i, (total, target))
    else:
        total, target = lax.fori_loop(0, steps, step, (total, target))
    sums = [jnp.broadcast_to(x, (images, 128)).T[:1] for x in (total, LOGIT_SCALE * target)]
    width = keep.shape[1]
    rows = [x[:, c : c + width] for x in sums for c in range(0, images, width)]
    rows = [jnp.pad(x, ((0, 0), (0, width - x.shape[1]))) for x in rows]
    rows = jnp.concatenate(rows + [jnp.zeros((8 - len(rows), width), F32)])
    for ref, part in ((keep, weighted[:group]), (send, weighted[group:])):
        ref[:group, :] = part
        ref[group:, :] = rows
    store.wait()


def softmax_sums(hid_a, hid_b, second, marks, classes, half):
    width = half.shape[1]
    group = hid_a.shape[0]
    images = marks.shape[1]
    steps = classes.shape[0]
    count = classes.size
    return pl.pallas_call(
        functools.partial(softmax_kernel, images <= 256),
        in_specs=[HBM] * 3 + [VMEM] * 2 + [HBM],
        out_specs=[VMEM] * 2 + [HBM],
        input_output_aliases={5: 2},
        out_shape=[
            jax.ShapeDtypeStruct((group + 8, width), F32),
            jax.ShapeDtypeStruct((group + 8, width), F32),
            jax.ShapeDtypeStruct(half.shape, BF16),
        ],
        scratch_shapes=[
            pltpu.VMEM(hid_a.shape, BF16),
            pltpu.VMEM(hid_b.shape, BF16),
            pltpu.VMEM(second.shape, BF16),
            pltpu.VMEM((count, width), BF16),
            pltpu.VMEM((images, width), BF16),
            pltpu.VMEM((images, width), F32),
            pltpu.SemaphoreType.DMA((3,)),
            pltpu.SemaphoreType.DMA((steps,)),
            pltpu.SemaphoreType.DMA,
        ],
        compiler_params=params(40),
        cost_estimate=cost(4 * count * width * images, 4 * count * width),
    )(hid_a, hid_b, second, marks, classes, half)


def chunked(steps, tile, pairs, sem):
    def copies(i):
        rows = rows_at(i, tile)
        return [
            pltpu.make_async_copy(source.at[rows], target.at[rows], sem.at[p, i])
            for p, (source, target) in enumerate(pairs)
        ]

    def start(i):
        for copy in copies(i):
            copy.start()

    def wait(i):
        for copy in copies(i):
            copy.wait()

    return start, wait


def columns_of(classes):
    pad = jnp.zeros((-classes.shape[0] % 8, classes.shape[1]), jnp.int32)
    return jnp.concatenate([classes[...], pad]).T


def inverse_norm(block):
    return lax.rsqrt(jnp.sum(block * block, axis=1, keepdims=True) + NORM_EPSILON)


def terms_kernel(
    marks_hbm, classes_hbm, shared_hbm, out_hbm, marks, classes, half, unit, out, first_sem, in_sem, out_sem
):
    steps, tile = classes.shape
    count = steps * tile
    units = shared_hbm.at[pl.ds(count, unit.shape[0])]
    firsts = [
        pltpu.make_async_copy(source, place, first_sem.at[i])
        for i, (source, place) in enumerate(((marks_hbm, marks), (classes_hbm, classes), (units, unit)))
    ]
    for copy in firsts:
        copy.start()
    load, loaded = chunked(steps, tile, [(shared_hbm, half)], in_sem)
    store, stored = chunked(steps, tile, [(out, out_hbm)], out_sem)
    for i in range(min(AHEAD, steps)):
        load(i)
    for copy in firsts:
        copy.wait()
    columns = columns_of(classes)
    for i in range(steps):
        loaded(i)
        if i + AHEAD < steps:
            load(i + AHEAD)
        rows = rows_at(i, tile)
        cosine = dot(half[rows, :], unit[...], NT)
        positive = columns[:, i : i + 1] == marks[...]
        terms = exp_terms_of(cosine, positive)
        out[rows, :] = jnp.where(positive, -jnp.maximum(terms, SMALLEST), terms).astype(BF16)
        store(i)
    for i in range(steps):
        stored(i)


def turned_terms(classes, marks, shared):
    count, width = classes.size, shared.shape[1]
    images = marks.shape[1]
    steps = classes.shape[0]
    return pl.pallas_call(
        terms_kernel,
        in_specs=[HBM] * 3,
        out_specs=HBM,
        out_shape=jax.ShapeDtypeStruct((count, images), BF16),
        scratch_shapes=[
            pltpu.VMEM(marks.shape, jnp.int32),
            pltpu.VMEM(classes.shape, jnp.int32),
            pltpu.VMEM((count, width), BF16),
            pltpu.VMEM((images, width), BF16),
            pltpu.VMEM((count, images), BF16),
            pltpu.SemaphoreType.DMA((3,)),
            pltpu.SemaphoreType.DMA((1, steps)),
            pltpu.SemaphoreType.DMA((1, steps)),
        ],
        compiler_params=params(57),
        cost_estimate=cost(2 * count * width * images, 8 * count * width),
    )(marks, classes, shared)


def centres_kernel(
    factor,
    totals_hbm,
    cen_hbm,
    shared_hbm,
    terms_hbm,
    out_hbm,
    totals,
    unit,
    cen,
    terms,
    out,
    first_sem,
    in_sem,
    out_sem,
):
    steps = in_sem.shape[1]
    count = cen.shape[0]
    tile = count // steps
    firsts = [
        pltpu.make_async_copy(totals_hbm, totals, first_sem.at[0]),
        pltpu.make_async_copy(shared_hbm.at[pl.ds(count, unit.shape[0])], unit, first_sem.at[1]),
    ]
    load, loaded = chunked(steps, tile, [(cen_hbm, cen), (terms_hbm, terms)], in_sem)
    store, stored = chunked(steps, tile, [(out, out_hbm)], out_sem)
    for copy in firsts:
        copy.start()
    for i in range(min(AHEAD + 1, steps)):
        load(i)
    for copy in firsts:
        copy.wait()
    share = factor / totals[...]
    for i in range(steps):
        loaded(i)
        if i + AHEAD + 1 < steps:
            load(i + AHEAD + 1)
        rows = rows_at(i, tile)
        block = cen[rows, :].astype(F32)
        inv = inverse_norm(block)
        signed = terms[rows, :].astype(F32)
        coeff = jnp.abs(signed) * share - jnp.where(signed < 0.0, factor, 0.0)
        grad = dot(coeff.astype(BF16), unit[...])
        along = jnp.sum(grad * block, axis=1, keepdims=True) * (inv * inv)
        out[rows, :] = (inv * (grad - block * along)).astype(BF16)
        store(i)
    for i in range(steps):
        stored(i)


def grad_centres(centres, terms, shared, totals):
    count, width = centres.shape
    images = terms.shape[1]
    steps = count // tile_of(count, 640)
    return pl.pallas_call(
        functools.partial(centres_kernel, LOGIT_SCALE / images),
        in_specs=[HBM] * 4,
        out_specs=HBM,
        out_shape=jax.ShapeDtypeStruct((count, width), BF16),
        scratch_shapes=[
            pltpu.VMEM((1, images), F32),
            pltpu.VMEM((images, width), BF16),
            pltpu.VMEM((count, width), BF16),
            pltpu.VMEM((count, images), BF16),
            pltpu.VMEM((count, width), BF16),
            pltpu.SemaphoreType.DMA((2,)),
            pltpu.SemaphoreType.DMA((2, steps)),
            pltpu.SemaphoreType.DMA((1, steps)),
        ],
        compiler_params=params(57),
        cost_estimate=cost(4 * count * width * images, 8 * count * width),
    )(totals, centres, shared, terms)


def turn_kernel(rows, place_ref, *refs):
    blocks, out_ref, stack = refs[:-2], refs[-2], refs[-1]
    group, depth = blocks[0].shape
    y = place_ref[0]
    for i, block in enumerate(blocks):
        dy, dc = divmod(i, 2)
        where = dc * rows + lax.rem(y - dy + rows, rows)
        stack[pl.ds(pl.multiple_of(where * group, group), group), :] = block[...]
    width = tile_of(depth, 128)

    if width == 128:

        def turn(i, carry):
            columns = pl.ds(pl.multiple_of(i * width, width), width)
            out_ref[columns, :] = stack[:, columns].T
            return carry

        lax.fori_loop(0, depth // width, turn, 0)
    else:
        out_ref[...] = stack[...].T


def turned(rows, place, blocks):
    group, depth = blocks[0].shape
    images = group * len(blocks)
    return pl.pallas_call(
        functools.partial(turn_kernel, rows),
        in_specs=[pl.BlockSpec(memory_space=pltpu.SMEM)] + [VMEM] * len(blocks),
        out_specs=VMEM,
        out_shape=jax.ShapeDtypeStruct((depth, images), BF16),
        scratch_shapes=[pltpu.VMEM((images, depth), BF16)],
        compiler_params=params(57),
        cost_estimate=cost(0, 4 * depth * images),
    )(place, *blocks)


def tail_kernel(
    grad_a,
    grad_b,
    hid_a,
    hid_b,
    second,
    features,
    first_hbm,
    second_out,
    out,
    grad_hidden,
    out_sem,
):
    group = grad_a.shape[0]
    steps = out_sem.shape[0]
    tile = out.shape[0] // steps

    def store(i):
        rows = rows_at(i, tile)
        return pltpu.make_async_copy(out.at[rows], first_hbm.at[rows], out_sem.at[i])

    acts = []
    for place, (grad, hid) in enumerate(((grad_a, hid_a), (grad_b, hid_b))):
        act, slope = gelu_parts(hid[...].astype(F32))
        acts.append(act.astype(BF16))
        grad_act = dot(grad[...], second[...], NT)
        grad_hidden[pl.ds(place * group, group), :] = (grad_act * slope).astype(BF16)

    def step(i):
        rows = rows_at(i, tile)
        out[rows, :] = dot(features[rows, :], grad_hidden[...]).astype(BF16)
        store(i).start()

    each(steps, True, step)
    act = jnp.concatenate(acts)
    grad = jnp.concatenate([grad_a[...], grad_b[...]])
    second_out[...] = dot(act.T, grad).astype(BF16)
    each(steps, True, lambda i: store(i).wait())


def tail(grad_a, grad_b, hid_a, hid_b, second, turned_features):
    depth, images = turned_features.shape
    hidden, width = second.shape
    steps = depth // tile_of(depth, 600)
    return pl.pallas_call(
        tail_kernel,
        in_specs=[VMEM] * 6,
        out_specs=[HBM, VMEM],
        out_shape=[
            jax.ShapeDtypeStruct((depth, hidden), BF16),
            jax.ShapeDtypeStruct((hidden, width), BF16),
        ],
        scratch_shapes=[
            pltpu.VMEM((depth, hidden), BF16),
            pltpu.VMEM((images, hidden), BF16),
            pltpu.SemaphoreType.DMA((steps,)),
        ],
        compiler_params=params(40),
        cost_estimate=cost(2 * depth * hidden * images, 2 * depth * (hidden + images)),
    )(grad_a, grad_b, hid_a, hid_b, second, turned_features)


def assemble_kernel(images, keep, got, out):
    width = keep.shape[1]
    half = keep.shape[0] - 8
    each = -(-images // width)

    def sums(ref):
        lines = [
            jnp.concatenate([ref[half + each * q + r : half + each * q + r + 1, :] for r in range(each)], axis=1)
            for q in range(2)
        ]
        return jnp.concatenate(lines)[:, :images]

    other = sums(got)
    both = sums(keep) + jnp.concatenate([other[:, images // 2 :], other[:, : images // 2]], axis=1)
    scale = jnp.where(lax.broadcasted_iota(jnp.int32, both.shape, 0) == 0, PIECE_SCALE, 1.0)
    both = both * scale
    parts = []
    for _ in range(3):
        part = both.astype(BF16).astype(F32)
        parts.append(part)
        both = both - part
    riding = jnp.concatenate(parts + [jnp.zeros_like(both)])
    out[:, :width] = (keep[:half, :] + got[:half, :]).astype(BF16)
    out[:, width:] = jnp.concatenate([riding] * (half // 8)).astype(BF16)


def assemble(images, keep, got):
    half, width = keep.shape[0] - 8, keep.shape[1]
    return pl.pallas_call(
        functools.partial(assemble_kernel, images),
        in_specs=[VMEM] * 2,
        out_specs=VMEM,
        out_shape=jax.ShapeDtypeStruct((half, width + images), BF16),
        compiler_params=params(16),
        cost_estimate=cost(0, 8 * half * (width + images)),
    )(keep, got)


def core_swap(x):
    return lax.ppermute(x, "core", [(0, 1), (1, 0)])


def to_chips(x):
    return lax.all_to_all(x, ("row", "gy"), 0, 0, tiled=True)


def to_all_chips(x, chips):
    x = to_chips(jnp.broadcast_to(x[None], (chips,) + x.shape))
    return x.reshape(-1, x.shape[-1])


def shards(features, first_weight, second_weight, centres, active, labels):
    rows, gy_count = lax.axis_size("row"), lax.axis_size("gy")
    y, core, gy = lax.axis_index("row"), lax.axis_index("core"), lax.axis_index("gy")
    chips = rows * gy_count
    chip = y * gy_count + gy
    device = (y * 2 + core) * gy_count + gy
    image_count = labels.shape[0]
    half = image_count // 2
    group = features.shape[0]
    own = half // chips
    depth = first_weight.shape[0]

    blocks = {}
    others = list(range(1, rows))
    for dy, dc in [(dy, 1) for dy in others] + [(0, 1)] + [(dy, 0) for dy in others] + [(0, 0)]:
        target = ((y + dy) % rows) * 2 + (core ^ dc)
        if (dy, dc) == (0, 0):
            source, labels = lax.optimization_barrier((features, labels))
            blocks[dy, dc] = lax.dynamic_slice_in_dim(source, target * depth, depth, axis=1)
            continue
        part = lax.dynamic_slice_in_dim(features, target * depth, depth, axis=1)
        perm = [
            (a * 2 + b, ((a + dy) % rows) * 2 + (b ^ dc)) for a in range(rows) for b in range(2)
        ]
        blocks[dy, dc] = lax.ppermute(part, ("row", "core"), perm)

    marks = labels.reshape(rows, 2, group).transpose(1, 0, 2)
    marks = jnp.where(core == 0, marks, marks[::-1]).reshape(image_count)
    marks = marks[None, :]
    count = active.shape[0]
    tile = tile_of(count, 1280 if image_count <= 256 else 256)
    classes = (device * CLS_DEV + active).reshape(count // tile, tile)

    first_arrived, marks, classes = lax.optimization_barrier((blocks[0, 1], marks, classes))
    blocks[0, 1] = first_arrived
    normed_half, picked = prep(centres, marks, classes)
    picked = picked[:half] + core_swap(picked[half:])

    def partial_hidden(*names):
        return jnp.dot(
            jnp.concatenate([blocks[n] for n in names]), first_weight, preferred_element_type=F32
        )

    near = partial_hidden((0, 1), (0, 0))
    early = [blocks[dy, 1] for dy in others]
    early, near, normed_half, picked = lax.optimization_barrier((early, near, normed_half, picked))
    for dy, block in zip(others, early):
        blocks[dy, 1] = block
    far_send = partial_hidden(*[(dy, 1) for dy in others])
    near_keep = near[group:] + core_swap(near[:group])
    far_got = core_swap(far_send)
    last = [blocks[dy, 0] for dy in others]
    last, far_got, near_keep, picked = lax.optimization_barrier((last, far_got, near_keep, picked))
    for dy, block in zip(others, last):
        blocks[dy, 0] = block
    far_keep = partial_hidden(*[(dy, 0) for dy in others]) + far_got
    if rows == 2:
        part = jnp.where(
            y == 0,
            jnp.concatenate([near_keep, far_keep]),
            jnp.concatenate([far_keep, near_keep]),
        )
    else:
        part = jnp.concatenate([near_keep, far_keep]).reshape(rows, group, -1)
        part = part[(y - jnp.arange(rows)) % rows].reshape(half, -1)
    wide = part.shape[1]
    part = jnp.concatenate([part.astype(BF16), picked], axis=1)
    part = to_chips(part.reshape(chips, own, -1))
    place = jnp.reshape(y, (1,)).astype(jnp.int32)
    order = [(dy, dc) for dy in range(rows) for dc in range(2)]
    turned_features = turned(rows, place, [blocks[n] for n in order])
    part, turned_features = lax.optimization_barrier((part, turned_features))
    part = jnp.sum(part.astype(F32), axis=0)
    hidden_own, picked = part[:, :wide].astype(BF16), part[:, wide:]
    hid_a = to_all_chips(hidden_own, chips)
    hid_b = core_swap(hid_a)

    embed_own = jnp.dot(
        gelu_parts(hidden_own.astype(F32))[0].astype(BF16), second_weight, preferred_element_type=F32
    )
    inv_own = lax.rsqrt(jnp.sum(embed_own * embed_own, axis=1, keepdims=True) + NORM_EPSILON)
    unit_own = embed_own * inv_own

    weighted, weighted_send, shared = softmax_sums(
        hid_a, hid_b, second_weight, marks, classes, normed_half
    )
    width = weighted.shape[1]
    sent = assemble(image_count, weighted, core_swap(weighted_send))
    sent, shared = lax.optimization_barrier((sent, shared))
    terms = turned_terms(classes, marks, shared)
    sent, terms = lax.optimization_barrier((to_chips(sent.reshape(chips, own, -1)), terms))
    sent = jnp.sum(sent.astype(F32), axis=0)
    weighted = sent[:, :width]
    sums = sent[:, width:].reshape(4, 2, image_count).sum(axis=0)
    totals, target = sums[0:1] * (1.0 / PIECE_SCALE), sums[1:2]

    factor = LOGIT_SCALE / image_count
    totals_own = lax.dynamic_slice_in_dim(totals, chip * own, own, axis=1).reshape(own, 1)
    grad_unit = factor * (weighted / totals_own - picked)
    grad_embed = inv_own * (grad_unit - unit_own * jnp.sum(grad_unit * unit_own, axis=1, keepdims=True))
    grad_embed = grad_embed.astype(BF16)
    grad_embed = jnp.broadcast_to(grad_embed[None], (chips,) + grad_embed.shape)
    grad_embed, totals, target = lax.optimization_barrier((grad_embed, totals, target))
    grad_cen = grad_centres(centres, terms, shared, totals)
    grad_a = to_chips(grad_embed).reshape(half, -1)
    grad_a, grad_cen = lax.optimization_barrier((grad_a, grad_cen))
    grad_b = core_swap(grad_a)
    loss = jnp.mean(LOGIT_SCALE + jnp.log(totals) - target)
    grad_first, grad_second = tail(grad_a, grad_b, hid_a, hid_b, second_weight, turned_features)
    return loss, grad_first, grad_second, grad_cen


def solution(mesh):
    gx_count, gy_count = mesh.shape["gx"], mesh.shape["gy"]
    fine = Mesh(mesh.devices.reshape(gx_count // 2, 2, gy_count), ("row", "core", "gy"))
    gx = ("row", "core")
    placed = (
        P(gx, "gy"),
        P(("gy",) + gx, None),
        P(),
        P(gx + ("gy",), None),
        P(gx + ("gy",)),
        P(),
    )
    return jax.shard_map(
        shards,
        mesh=fine,
        in_specs=placed,
        out_specs=(P(), P(("gy",) + gx, None), P(), P(gx + ("gy",), None)),
        check_vma=False,
    )
```

```python
import functools

import jax
import jax.numpy as jnp
from jax import lax
from jax.experimental import pallas as pl
from jax.experimental.pallas import tpu as pltpu
from jax.sharding import Mesh, PartitionSpec as P

CLS_DEV = 16128


LOGIT_SCALE = 64.0
COS_MARGIN = 0.4
NORM_EPSILON = 1e-06

POWER = LOGIT_SCALE * 1.4426950408889634

PIECE_SCALE = 2.0**64

SMALLEST = 1.1754944e-38

AHEAD = 2

F32, BF16 = jnp.float32, jnp.bfloat16
MIB = 2**20
VMEM = pl.BlockSpec(memory_space=pltpu.VMEM)
HBM = pl.BlockSpec(memory_space=pltpu.HBM)

NN = (((1,), (0,)), ((), ()))
NT = (((1,), (1,)), ((), ()))


def dot(a, b, dims=NN):
    return lax.dot_general(a, b, dims, preferred_element_type=F32)


def tile_of(extent, most, unit=16):
    return max(t for t in range(unit, most + 1, unit) if extent % t == 0)


def gelu_parts(v):
    scale = 0.7978845608028654
    cube = 0.044715
    square = v * v
    bend = jnp.tanh(scale * (v + cube * square * v))
    left = 0.5 * (1.0 + bend)
    slope = left + 0.5 * v * (1.0 - bend * bend) * scale * (1.0 + 3.0 * cube * square)
    return v * left, slope


def row_to_column(row):
    return jnp.broadcast_to(row, (8, row.shape[1])).T[:, :1]


def each(count, plain, step):
    if plain:
        for i in range(count):
            step(i)
    else:

        def run(i, carry):
            step(i)
            return carry

        lax.fori_loop(0, count, run, 0)


def rows_at(i, tile):
    return pl.ds(i * tile if isinstance(i, int) else pl.multiple_of(i * tile, tile), tile)


def params(mib):
    return pltpu.CompilerParams(vmem_limit_bytes=mib * MIB)


def cost(flops, moved):
    return pl.CostEstimate(flops=flops, bytes_accessed=moved, transcendentals=0)


def exp_terms_of(cosine, positive):
    return jnp.exp2(
        cosine * POWER - jnp.where(positive, POWER * (1.0 + COS_MARGIN), POWER)
    )


def prep_kernel(plain, marks, classes, cen_hbm, half_hbm, picked, cen, half, total, in_sem, out_sem):
    steps, tile = classes.shape
    column = row_to_column(marks[...])

    def load(i):
        rows = rows_at(i, tile)
        return pltpu.make_async_copy(cen_hbm.at[rows], cen.at[rows], in_sem.at[i])

    def store(i):
        rows = rows_at(i, tile)
        return pltpu.make_async_copy(half.at[rows], half_hbm.at[rows], out_sem.at[i])

    each(steps, plain, lambda i: load(i).start())
    total[...] = jnp.zeros_like(total)

    def step(i):
        load(i).wait()
        rows = rows_at(i, tile)
        block = cen[rows, :].astype(F32)
        inv = lax.rsqrt(jnp.sum(block * block, axis=1, keepdims=True) + NORM_EPSILON)
        block = (block * inv).astype(BF16)
        half[rows, :] = block
        store(i).start()
        match = jnp.where(column == classes[pl.ds(i, 1), :], 1.0, 0.0).astype(BF16)
        total[...] += dot(match, block)

    each(steps, plain, step)
    picked[...] = total[...].astype(BF16)
    each(steps, plain, lambda i: store(i).wait())


def prep(centres, marks, classes):
    count, width = centres.shape
    images = marks.shape[1]
    steps = classes.shape[0]
    return pl.pallas_call(
        functools.partial(prep_kernel, images <= 256),
        in_specs=[VMEM, VMEM, HBM],
        out_specs=[HBM, VMEM],
        out_shape=[
            jax.ShapeDtypeStruct((5 * count, width), BF16),
            jax.ShapeDtypeStruct((images, width), BF16),
        ],
        scratch_shapes=[
            pltpu.VMEM((count, width), BF16),
            pltpu.VMEM((count, width), BF16),
            pltpu.VMEM((images, width), F32),
            pltpu.SemaphoreType.DMA((steps,)),
            pltpu.SemaphoreType.DMA((steps,)),
        ],
        compiler_params=params(28),
        cost_estimate=cost(2 * count * width * images, 8 * count * width),
    )(marks, classes, centres)


def softmax_kernel(
    plain,
    hid_a_hbm,
    hid_b_hbm,
    second_hbm,
    marks,
    classes,
    half_hbm,
    keep,
    send,
    shared,
    hid_a,
    hid_b,
    second,
    half,
    unit,
    weighted,
    first_sem,
    in_sem,
    out_sem,
):
    steps, tile = classes.shape
    firsts = [
        pltpu.make_async_copy(source, place, first_sem.at[i])
        for i, (source, place) in enumerate(
            ((hid_a_hbm, hid_a), (second_hbm, second), (hid_b_hbm, hid_b))
        )
    ]
    for copy in firsts:
        copy.start()

    def load(i):
        rows = rows_at(i, tile)
        return pltpu.make_async_copy(half_hbm.at[rows], half.at[rows], in_sem.at[i])

    load(0).start()
    group = hid_a.shape[0]
    images = 2 * group
    column = row_to_column(marks[...])
    firsts[0].wait()
    firsts[1].wait()
    each(steps - 1, plain, lambda i: load(i + 1).start())
    for place, hid in enumerate((hid_a, hid_b)):
        if place == 1:
            firsts[2].wait()
        act, _ = gelu_parts(hid[...].astype(F32))
        embedding = dot(act.astype(BF16), second[...])
        inv = lax.rsqrt(jnp.sum(embedding * embedding, axis=1, keepdims=True) + NORM_EPSILON)
        unit[pl.ds(place * group, group), :] = (embedding * inv).astype(BF16)
    store = pltpu.make_async_copy(unit, shared.at[pl.ds(steps * tile, images)], out_sem)
    store.start()
    weighted[...] = jnp.zeros_like(weighted)

    def step(i, sums):
        load(i).wait()
        block = half[rows_at(i, tile), :]
        cosine = dot(unit[...], block, NT)
        positive = column == classes[pl.ds(i, 1), :]
        exp_terms = exp_terms_of(cosine, positive)
        weighted[...] += dot(exp_terms.astype(BF16), block)
        total = jnp.sum(exp_terms, axis=1, keepdims=True)
        target = jnp.sum(jnp.where(positive, cosine - COS_MARGIN, 0.0), axis=1, keepdims=True)
        return sums[0] + total, sums[1] + target

    total = target = jnp.zeros((images, 1), F32)
    if plain:
        for i in range(steps):
            total, target = step(i, (total, target))
    else:
        total, target = lax.fori_loop(0, steps, step, (total, target))
    sums = [jnp.broadcast_to(x, (images, 128)).T[:1] for x in (total, LOGIT_SCALE * target)]
    width = keep.shape[1]
    rows = [x[:, c : c + width] for x in sums for c in range(0, images, width)]
    rows = [jnp.pad(x, ((0, 0), (0, width - x.shape[1]))) for x in rows]
    rows = jnp.concatenate(rows + [jnp.zeros((8 - len(rows), width), F32)])
    for ref, part in ((keep, weighted[:group]), (send, weighted[group:])):
        ref[:group, :] = part
        ref[group:, :] = rows
    store.wait()


def softmax_sums(hid_a, hid_b, second, marks, classes, half):
    width = half.shape[1]
    group = hid_a.shape[0]
    images = marks.shape[1]
    steps = classes.shape[0]
    count = classes.size
    return pl.pallas_call(
        functools.partial(softmax_kernel, images <= 256),
        in_specs=[HBM] * 3 + [VMEM] * 2 + [HBM],
        out_specs=[VMEM] * 2 + [HBM],
        input_output_aliases={5: 2},
        out_shape=[
            jax.ShapeDtypeStruct((group + 8, width), F32),
            jax.ShapeDtypeStruct((group + 8, width), F32),
            jax.ShapeDtypeStruct(half.shape, BF16),
        ],
        scratch_shapes=[
            pltpu.VMEM(hid_a.shape, BF16),
            pltpu.VMEM(hid_b.shape, BF16),
            pltpu.VMEM(second.shape, BF16),
            pltpu.VMEM((count, width), BF16),
            pltpu.VMEM((images, width), BF16),
            pltpu.VMEM((images, width), F32),
            pltpu.SemaphoreType.DMA((3,)),
            pltpu.SemaphoreType.DMA((steps,)),
            pltpu.SemaphoreType.DMA,
        ],
        compiler_params=params(40),
        cost_estimate=cost(4 * count * width * images, 4 * count * width),
    )(hid_a, hid_b, second, marks, classes, half)


def chunked(steps, tile, pairs, sem):
    def copies(i):
        rows = rows_at(i, tile)
        return [
            pltpu.make_async_copy(source.at[rows], target.at[rows], sem.at[p, i])
            for p, (source, target) in enumerate(pairs)
        ]

    def start(i):
        for copy in copies(i):
            copy.start()

    def wait(i):
        for copy in copies(i):
            copy.wait()

    return start, wait


def columns_of(classes):
    pad = jnp.zeros((-classes.shape[0] % 8, classes.shape[1]), jnp.int32)
    return jnp.concatenate([classes[...], pad]).T


def inverse_norm(block):
    return lax.rsqrt(jnp.sum(block * block, axis=1, keepdims=True) + NORM_EPSILON)


def terms_kernel(
    marks_hbm, classes_hbm, shared_hbm, out_hbm, marks, classes, half, unit, out, first_sem, in_sem, out_sem
):
    steps, tile = classes.shape
    count = steps * tile
    units = shared_hbm.at[pl.ds(count, unit.shape[0])]
    firsts = [
        pltpu.make_async_copy(source, place, first_sem.at[i])
        for i, (source, place) in enumerate(((marks_hbm, marks), (classes_hbm, classes), (units, unit)))
    ]
    for copy in firsts:
        copy.start()
    load, loaded = chunked(steps, tile, [(shared_hbm, half)], in_sem)
    store, stored = chunked(steps, tile, [(out, out_hbm)], out_sem)
    for i in range(min(AHEAD, steps)):
        load(i)
    for copy in firsts:
        copy.wait()
    columns = columns_of(classes)
    for i in range(steps):
        loaded(i)
        if i + AHEAD < steps:
            load(i + AHEAD)
        rows = rows_at(i, tile)
        cosine = dot(half[rows, :], unit[...], NT)
        positive = columns[:, i : i + 1] == marks[...]
        terms = exp_terms_of(cosine, positive)
        out[rows, :] = jnp.where(positive, -jnp.maximum(terms, SMALLEST), terms).astype(BF16)
        store(i)
    for i in range(steps):
        stored(i)


def turned_terms(classes, marks, shared):
    count, width = classes.size, shared.shape[1]
    images = marks.shape[1]
    steps = classes.shape[0]
    return pl.pallas_call(
        terms_kernel,
        in_specs=[HBM] * 3,
        out_specs=HBM,
        out_shape=jax.ShapeDtypeStruct((count, images), BF16),
        scratch_shapes=[
            pltpu.VMEM(marks.shape, jnp.int32),
            pltpu.VMEM(classes.shape, jnp.int32),
            pltpu.VMEM((count, width), BF16),
            pltpu.VMEM((images, width), BF16),
            pltpu.VMEM((count, images), BF16),
            pltpu.SemaphoreType.DMA((3,)),
            pltpu.SemaphoreType.DMA((1, steps)),
            pltpu.SemaphoreType.DMA((1, steps)),
        ],
        compiler_params=params(57),
        cost_estimate=cost(2 * count * width * images, 8 * count * width),
    )(marks, classes, shared)


def centres_kernel(
    factor,
    sums_hbm,
    cen_hbm,
    shared_hbm,
    terms_hbm,
    out_hbm,
    loss,
    sums,
    unit,
    cen,
    terms,
    out,
    first_sem,
    in_sem,
    out_sem,
):
    steps = in_sem.shape[1]
    count = cen.shape[0]
    tile = count // steps
    firsts = [
        pltpu.make_async_copy(sums_hbm, sums, first_sem.at[0]),
        pltpu.make_async_copy(shared_hbm.at[pl.ds(count, unit.shape[0])], unit, first_sem.at[1]),
    ]
    load, loaded = chunked(steps, tile, [(cen_hbm, cen), (terms_hbm, terms)], in_sem)
    store, stored = chunked(steps, tile, [(out, out_hbm)], out_sem)
    for copy in firsts:
        copy.start()
    for i in range(min(AHEAD + 1, steps)):
        load(i)
    for copy in firsts:
        copy.wait()
    totals, target = sums[0:1, :] * (1.0 / PIECE_SCALE), sums[1:2, :]
    share = factor / totals
    for i in range(steps):
        loaded(i)
        if i + AHEAD + 1 < steps:
            load(i + AHEAD + 1)
        rows = rows_at(i, tile)
        block = cen[rows, :].astype(F32)
        inv = inverse_norm(block)
        signed = terms[rows, :].astype(F32)
        coeff = jnp.abs(signed) * share - jnp.where(signed < 0.0, factor, 0.0)
        grad = dot(coeff.astype(BF16), unit[...])
        along = jnp.sum(grad * block, axis=1, keepdims=True) * (inv * inv)
        out[rows, :] = (inv * (grad - block * along)).astype(BF16)
        store(i)
    loss[0, 0] = jnp.sum(LOGIT_SCALE + jnp.log(totals) - target) / totals.shape[1]
    for i in range(steps):
        stored(i)


def grad_centres(centres, terms, shared, sums):
    count, width = centres.shape
    images = terms.shape[1]
    steps = count // tile_of(count, 640)
    return pl.pallas_call(
        functools.partial(centres_kernel, LOGIT_SCALE / images),
        in_specs=[HBM] * 4,
        out_specs=[HBM, pl.BlockSpec(memory_space=pltpu.SMEM)],
        out_shape=[
            jax.ShapeDtypeStruct((count, width), BF16),
            jax.ShapeDtypeStruct((1, 1), F32),
        ],
        scratch_shapes=[
            pltpu.VMEM((2, images), F32),
            pltpu.VMEM((images, width), BF16),
            pltpu.VMEM((count, width), BF16),
            pltpu.VMEM((count, images), BF16),
            pltpu.VMEM((count, width), BF16),
            pltpu.SemaphoreType.DMA((2,)),
            pltpu.SemaphoreType.DMA((2, steps)),
            pltpu.SemaphoreType.DMA((1, steps)),
        ],
        compiler_params=params(57),
        cost_estimate=cost(4 * count * width * images, 8 * count * width),
    )(sums, centres, shared, terms)


def turn_kernel(rows, place_ref, *refs):
    blocks, out_ref, stack = refs[:-2], refs[-2], refs[-1]
    group, depth = blocks[0].shape
    y = place_ref[0]
    for i, block in enumerate(blocks):
        dy, dc = divmod(i, 2)
        where = dc * rows + lax.rem(y - dy + rows, rows)
        stack[pl.ds(pl.multiple_of(where * group, group), group), :] = block[...]
    width = tile_of(depth, 128)

    if width == 128:

        def turn(i, carry):
            columns = pl.ds(pl.multiple_of(i * width, width), width)
            out_ref[columns, :] = stack[:, columns].T
            return carry

        lax.fori_loop(0, depth // width, turn, 0)
    else:
        out_ref[...] = stack[...].T


def turned(rows, place, blocks):
    group, depth = blocks[0].shape
    images = group * len(blocks)
    return pl.pallas_call(
        functools.partial(turn_kernel, rows),
        in_specs=[pl.BlockSpec(memory_space=pltpu.SMEM)] + [VMEM] * len(blocks),
        out_specs=VMEM,
        out_shape=jax.ShapeDtypeStruct((depth, images), BF16),
        scratch_shapes=[pltpu.VMEM((images, depth), BF16)],
        compiler_params=params(57),
        cost_estimate=cost(0, 4 * depth * images),
    )(place, *blocks)


def tail_kernel(
    grad_a,
    grad_b,
    hid_a,
    hid_b,
    second,
    features,
    first_hbm,
    second_out,
    out,
    grad_hidden,
    out_sem,
):
    group = grad_a.shape[0]
    steps = out_sem.shape[0]
    tile = out.shape[0] // steps

    def store(i):
        rows = rows_at(i, tile)
        return pltpu.make_async_copy(out.at[rows], first_hbm.at[rows], out_sem.at[i])

    acts = []
    for place, (grad, hid) in enumerate(((grad_a, hid_a), (grad_b, hid_b))):
        act, slope = gelu_parts(hid[...].astype(F32))
        acts.append(act.astype(BF16))
        grad_act = dot(grad[...], second[...], NT)
        grad_hidden[pl.ds(place * group, group), :] = (grad_act * slope).astype(BF16)

    def step(i):
        rows = rows_at(i, tile)
        out[rows, :] = dot(features[rows, :], grad_hidden[...]).astype(BF16)
        store(i).start()

    each(steps, True, step)
    act = jnp.concatenate(acts)
    grad = jnp.concatenate([grad_a[...], grad_b[...]])
    second_out[...] = dot(act.T, grad).astype(BF16)
    each(steps, True, lambda i: store(i).wait())


def tail(grad_a, grad_b, hid_a, hid_b, second, turned_features):
    depth, images = turned_features.shape
    hidden, width = second.shape
    steps = depth // tile_of(depth, 600)
    return pl.pallas_call(
        tail_kernel,
        in_specs=[VMEM] * 6,
        out_specs=[HBM, VMEM],
        out_shape=[
            jax.ShapeDtypeStruct((depth, hidden), BF16),
            jax.ShapeDtypeStruct((hidden, width), BF16),
        ],
        scratch_shapes=[
            pltpu.VMEM((depth, hidden), BF16),
            pltpu.VMEM((images, hidden), BF16),
            pltpu.SemaphoreType.DMA((steps,)),
        ],
        compiler_params=params(40),
        cost_estimate=cost(2 * depth * hidden * images, 2 * depth * (hidden + images)),
    )(grad_a, grad_b, hid_a, hid_b, second, turned_features)


def assemble_kernel(images, keep, got, picked, out):
    width = keep.shape[1]
    half = keep.shape[0] - 8
    each = -(-images // width)

    def sums(ref):
        lines = [
            jnp.concatenate([ref[half + each * q + r : half + each * q + r + 1, :] for r in range(each)], axis=1)
            for q in range(2)
        ]
        return jnp.concatenate(lines)[:, :images]

    other = sums(got)
    both = sums(keep) + jnp.concatenate([other[:, images // 2 :], other[:, : images // 2]], axis=1)
    scale = jnp.where(lax.broadcasted_iota(jnp.int32, both.shape, 0) == 0, PIECE_SCALE, 1.0)
    both = both * scale
    parts = []
    for _ in range(3):
        part = both.astype(BF16).astype(F32)
        parts.append(part)
        both = both - part
    riding = jnp.concatenate(parts + [jnp.zeros_like(both)])
    out[:, :width] = (keep[:half, :] + got[:half, :]).astype(BF16)
    out[:, width : width + images] = jnp.concatenate([riding] * (half // 8)).astype(BF16)
    out[:, width + images :] = picked[...]


def assemble(images, keep, got, picked):
    half, width = keep.shape[0] - 8, keep.shape[1]
    return pl.pallas_call(
        functools.partial(assemble_kernel, images),
        in_specs=[VMEM] * 3,
        out_specs=VMEM,
        out_shape=jax.ShapeDtypeStruct((half, width + images + picked.shape[1]), BF16),
        compiler_params=params(16),
        cost_estimate=cost(0, 8 * half * (width + images)),
    )(keep, got, picked)


def core_swap(x):
    return lax.ppermute(x, "core", [(0, 1), (1, 0)])


def to_chips(x):
    return lax.all_to_all(x, ("row", "gy"), 0, 0, tiled=True)


def to_all_chips(x, chips):
    x = to_chips(jnp.broadcast_to(x[None], (chips,) + x.shape))
    return x.reshape(-1, x.shape[-1])


def shards(features, first_weight, second_weight, centres, active, labels):
    rows, gy_count = lax.axis_size("row"), lax.axis_size("gy")
    y, core, gy = lax.axis_index("row"), lax.axis_index("core"), lax.axis_index("gy")
    chips = rows * gy_count
    chip = y * gy_count + gy
    device = (y * 2 + core) * gy_count + gy
    image_count = labels.shape[0]
    half = image_count // 2
    group = features.shape[0]
    own = half // chips
    depth = first_weight.shape[0]

    blocks = {}
    others = list(range(1, rows))
    for dy, dc in [(dy, 1) for dy in others] + [(0, 1)] + [(dy, 0) for dy in others] + [(0, 0)]:
        target = ((y + dy) % rows) * 2 + (core ^ dc)
        if (dy, dc) == (0, 0):
            source, labels = lax.optimization_barrier((features, labels))
            blocks[dy, dc] = lax.dynamic_slice_in_dim(source, target * depth, depth, axis=1)
            continue
        part = lax.dynamic_slice_in_dim(features, target * depth, depth, axis=1)
        perm = [
            (a * 2 + b, ((a + dy) % rows) * 2 + (b ^ dc)) for a in range(rows) for b in range(2)
        ]
        blocks[dy, dc] = lax.ppermute(part, ("row", "core"), perm)

    marks = labels.reshape(rows, 2, group).transpose(1, 0, 2)
    marks = jnp.where(core == 0, marks, marks[::-1]).reshape(image_count)
    marks = marks[None, :]
    count = active.shape[0]
    tile = tile_of(count, 1280 if image_count <= 256 else 256)
    classes = (device * CLS_DEV + active).reshape(count // tile, tile)

    first_arrived, marks, classes = lax.optimization_barrier((blocks[0, 1], marks, classes))
    blocks[0, 1] = first_arrived
    normed_half, picked = prep(centres, marks, classes)
    picked = picked[:half] + core_swap(picked[half:])

    def partial_hidden(*names):
        return jnp.dot(
            jnp.concatenate([blocks[n] for n in names]), first_weight, preferred_element_type=F32
        )

    near = partial_hidden((0, 1), (0, 0))
    early = [blocks[dy, 1] for dy in others]
    early, near, normed_half, picked = lax.optimization_barrier((early, near, normed_half, picked))
    for dy, block in zip(others, early):
        blocks[dy, 1] = block
    far_send = partial_hidden(*[(dy, 1) for dy in others])
    near_keep = near[group:] + core_swap(near[:group])
    far_got = core_swap(far_send)
    last = [blocks[dy, 0] for dy in others]
    last, far_got, near_keep, picked = lax.optimization_barrier((last, far_got, near_keep, picked))
    for dy, block in zip(others, last):
        blocks[dy, 0] = block
    far_keep = partial_hidden(*[(dy, 0) for dy in others]) + far_got
    if rows == 2:
        part = jnp.where(
            y == 0,
            jnp.concatenate([near_keep, far_keep]),
            jnp.concatenate([far_keep, near_keep]),
        )
    else:
        part = jnp.concatenate([near_keep, far_keep]).reshape(rows, group, -1)
        part = part[(y - jnp.arange(rows)) % rows].reshape(half, -1)
    wide = part.shape[1]
    part = part.astype(BF16)
    part = to_chips(part.reshape(chips, own, -1))
    place = jnp.reshape(y, (1,)).astype(jnp.int32)
    order = [(dy, dc) for dy in range(rows) for dc in range(2)]
    turned_features = turned(rows, place, [blocks[n] for n in order])
    part, turned_features = lax.optimization_barrier((part, turned_features))
    part = jnp.sum(part.astype(F32), axis=0)
    hidden_own = part.astype(BF16)
    hid_a = to_all_chips(hidden_own, chips)
    hid_b = core_swap(hid_a)

    embed_own = jnp.dot(
        gelu_parts(hidden_own.astype(F32))[0].astype(BF16), second_weight, preferred_element_type=F32
    )
    inv_own = lax.rsqrt(jnp.sum(embed_own * embed_own, axis=1, keepdims=True) + NORM_EPSILON)
    unit_own = embed_own * inv_own

    weighted, weighted_send, shared = softmax_sums(
        hid_a, hid_b, second_weight, marks, classes, normed_half
    )
    width = weighted.shape[1]
    sent = assemble(image_count, weighted, core_swap(weighted_send), picked)
    sent, shared = lax.optimization_barrier((sent, shared))
    terms = turned_terms(classes, marks, shared)
    sent, terms = lax.optimization_barrier((to_chips(sent.reshape(chips, own, -1)), terms))
    sent = jnp.sum(sent.astype(F32), axis=0)
    weighted, riding = sent[:, :width], sent[:, width : width + image_count]
    picked = sent[:, width + image_count :]
    sums = riding.reshape(4, 2, image_count).sum(axis=0)
    totals = sums[0:1] * (1.0 / PIECE_SCALE)

    factor = LOGIT_SCALE / image_count
    totals_own = lax.dynamic_slice_in_dim(totals, chip * own, own, axis=1).reshape(own, 1)
    grad_unit = factor * (weighted / totals_own - picked)
    grad_embed = inv_own * (grad_unit - unit_own * jnp.sum(grad_unit * unit_own, axis=1, keepdims=True))
    grad_embed = grad_embed.astype(BF16)
    grad_embed = jnp.broadcast_to(grad_embed[None], (chips,) + grad_embed.shape)
    grad_cen, loss = grad_centres(centres, terms, shared, sums)
    grad_a = to_chips(grad_embed).reshape(half, -1)
    grad_a, grad_cen = lax.optimization_barrier((grad_a, grad_cen))
    grad_b = core_swap(grad_a)
    grad_first, grad_second = tail(grad_a, grad_b, hid_a, hid_b, second_weight, turned_features)
    return loss.reshape(()), grad_first, grad_second, grad_cen


def solution(mesh):
    gx_count, gy_count = mesh.shape["gx"], mesh.shape["gy"]
    fine = Mesh(mesh.devices.reshape(gx_count // 2, 2, gy_count), ("row", "core", "gy"))
    gx = ("row", "core")
    placed = (
        P(gx, "gy"),
        P(("gy",) + gx, None),
        P(),
        P(gx + ("gy",), None),
        P(gx + ("gy",)),
        P(),
    )
    return jax.shard_map(
        shards,
        mesh=fine,
        in_specs=placed,
        out_specs=(P(), P(("gy",) + gx, None), P(), P(gx + ("gy",), None)),
        check_vma=False,
    )
```

```python
import functools

import jax
import jax.numpy as jnp
from jax import lax
from jax.experimental import pallas as pl
from jax.experimental.pallas import tpu as pltpu
from jax.sharding import Mesh, PartitionSpec as P

CLS_DEV = 16128


LOGIT_SCALE = 64.0
COS_MARGIN = 0.4
NORM_EPSILON = 1e-06

POWER = LOGIT_SCALE * 1.4426950408889634

PIECE_SCALE = 2.0**64

SMALLEST = 1.1754944e-38

AHEAD = 2

F32, BF16 = jnp.float32, jnp.bfloat16
MIB = 2**20
VMEM = pl.BlockSpec(memory_space=pltpu.VMEM)
HBM = pl.BlockSpec(memory_space=pltpu.HBM)

NN = (((1,), (0,)), ((), ()))
NT = (((1,), (1,)), ((), ()))


def dot(a, b, dims=NN):
    return lax.dot_general(a, b, dims, preferred_element_type=F32)


def tile_of(extent, most, unit=16):
    return max(t for t in range(unit, most + 1, unit) if extent % t == 0)


def gelu_parts(v):
    scale = 0.7978845608028654
    cube = 0.044715
    square = v * v
    bend = jnp.tanh(scale * (v + cube * square * v))
    left = 0.5 * (1.0 + bend)
    slope = left + 0.5 * v * (1.0 - bend * bend) * scale * (1.0 + 3.0 * cube * square)
    return v * left, slope


def row_to_column(row):
    return jnp.broadcast_to(row, (8, row.shape[1])).T[:, :1]


def each(count, plain, step):
    if plain:
        for i in range(count):
            step(i)
    else:

        def run(i, carry):
            step(i)
            return carry

        lax.fori_loop(0, count, run, 0)


def rows_at(i, tile):
    return pl.ds(i * tile if isinstance(i, int) else pl.multiple_of(i * tile, tile), tile)


def params(mib):
    return pltpu.CompilerParams(vmem_limit_bytes=mib * MIB)


def cost(flops, moved):
    return pl.CostEstimate(flops=flops, bytes_accessed=moved, transcendentals=0)


def exp_terms_of(cosine, positive):
    return jnp.exp2(
        cosine * POWER - jnp.where(positive, POWER * (1.0 + COS_MARGIN), POWER)
    )


def prep_kernel(plain, marks, classes, cen_hbm, half_hbm, picked, cen, half, total, in_sem, out_sem):
    steps, tile = classes.shape
    column = row_to_column(marks[...])

    def load(i):
        rows = rows_at(i, tile)
        return pltpu.make_async_copy(cen_hbm.at[rows], cen.at[rows], in_sem.at[i])

    def store(i):
        rows = rows_at(i, tile)
        return pltpu.make_async_copy(half.at[rows], half_hbm.at[rows], out_sem.at[i])

    each(steps, plain, lambda i: load(i).start())
    total[...] = jnp.zeros_like(total)

    def step(i):
        load(i).wait()
        rows = rows_at(i, tile)
        block = cen[rows, :].astype(F32)
        inv = lax.rsqrt(jnp.sum(block * block, axis=1, keepdims=True) + NORM_EPSILON)
        block = (block * inv).astype(BF16)
        half[rows, :] = block
        store(i).start()
        match = jnp.where(column == classes[pl.ds(i, 1), :], 1.0, 0.0).astype(BF16)
        total[...] += dot(match, block)

    each(steps, plain, step)
    picked[...] = total[...].astype(BF16)
    each(steps, plain, lambda i: store(i).wait())


def prep(centres, marks, classes):
    count, width = centres.shape
    images = marks.shape[1]
    steps = classes.shape[0]
    return pl.pallas_call(
        functools.partial(prep_kernel, images <= 256),
        in_specs=[VMEM, VMEM, HBM],
        out_specs=[HBM, VMEM],
        out_shape=[
            jax.ShapeDtypeStruct((5 * count, width), BF16),
            jax.ShapeDtypeStruct((images, width), BF16),
        ],
        scratch_shapes=[
            pltpu.VMEM((count, width), BF16),
            pltpu.VMEM((count, width), BF16),
            pltpu.VMEM((images, width), F32),
            pltpu.SemaphoreType.DMA((steps,)),
            pltpu.SemaphoreType.DMA((steps,)),
        ],
        compiler_params=params(28),
        cost_estimate=cost(2 * count * width * images, 8 * count * width),
    )(marks, classes, centres)


def softmax_kernel(
    plain,
    hid_a_hbm,
    hid_b_hbm,
    second_hbm,
    marks,
    classes,
    half_hbm,
    keep,
    send,
    shared,
    hid_a,
    hid_b,
    second,
    half,
    unit,
    weighted,
    first_sem,
    in_sem,
    out_sem,
):
    steps, tile = classes.shape
    firsts = [
        pltpu.make_async_copy(source, place, first_sem.at[i])
        for i, (source, place) in enumerate(
            ((hid_a_hbm, hid_a), (second_hbm, second), (hid_b_hbm, hid_b))
        )
    ]
    for copy in firsts:
        copy.start()

    def load(i):
        rows = rows_at(i, tile)
        return pltpu.make_async_copy(half_hbm.at[rows], half.at[rows], in_sem.at[i])

    load(0).start()
    group = hid_a.shape[0]
    images = 2 * group
    column = row_to_column(marks[...])
    firsts[0].wait()
    firsts[1].wait()
    each(steps - 1, plain, lambda i: load(i + 1).start())
    for place, hid in enumerate((hid_a, hid_b)):
        if place == 1:
            firsts[2].wait()
        act, _ = gelu_parts(hid[...].astype(F32))
        embedding = dot(act.astype(BF16), second[...])
        inv = lax.rsqrt(jnp.sum(embedding * embedding, axis=1, keepdims=True) + NORM_EPSILON)
        unit[pl.ds(place * group, group), :] = (embedding * inv).astype(BF16)
    store = pltpu.make_async_copy(unit, shared.at[pl.ds(steps * tile, images)], out_sem)
    store.start()
    weighted[...] = jnp.zeros_like(weighted)

    def step(i, sums):
        load(i).wait()
        block = half[rows_at(i, tile), :]
        cosine = dot(unit[...], block, NT)
        positive = column == classes[pl.ds(i, 1), :]
        exp_terms = exp_terms_of(cosine, positive)
        weighted[...] += dot(exp_terms.astype(BF16), block)
        total = jnp.sum(exp_terms, axis=1, keepdims=True)
        target = jnp.sum(jnp.where(positive, cosine - COS_MARGIN, 0.0), axis=1, keepdims=True)
        return sums[0] + total, sums[1] + target

    total = target = jnp.zeros((images, 1), F32)
    if plain:
        for i in range(steps):
            total, target = step(i, (total, target))
    else:
        total, target = lax.fori_loop(0, steps, step, (total, target))
    sums = [jnp.broadcast_to(x, (images, 128)).T[:1] for x in (total, LOGIT_SCALE * target)]
    width = keep.shape[1]
    rows = [x[:, c : c + width] for x in sums for c in range(0, images, width)]
    rows = [jnp.pad(x, ((0, 0), (0, width - x.shape[1]))) for x in rows]
    rows = jnp.concatenate(rows + [jnp.zeros((8 - len(rows), width), F32)])
    for ref, part in ((keep, weighted[:group]), (send, weighted[group:])):
        ref[:group, :] = part
        ref[group:, :] = rows
    store.wait()


def softmax_sums(hid_a, hid_b, second, marks, classes, half):
    width = half.shape[1]
    group = hid_a.shape[0]
    images = marks.shape[1]
    steps = classes.shape[0]
    count = classes.size
    return pl.pallas_call(
        functools.partial(softmax_kernel, images <= 256),
        in_specs=[HBM] * 3 + [VMEM] * 2 + [HBM],
        out_specs=[VMEM] * 2 + [HBM],
        input_output_aliases={5: 2},
        out_shape=[
            jax.ShapeDtypeStruct((group + 8, width), F32),
            jax.ShapeDtypeStruct((group + 8, width), F32),
            jax.ShapeDtypeStruct(half.shape, BF16),
        ],
        scratch_shapes=[
            pltpu.VMEM(hid_a.shape, BF16),
            pltpu.VMEM(hid_b.shape, BF16),
            pltpu.VMEM(second.shape, BF16),
            pltpu.VMEM((count, width), BF16),
            pltpu.VMEM((images, width), BF16),
            pltpu.VMEM((images, width), F32),
            pltpu.SemaphoreType.DMA((3,)),
            pltpu.SemaphoreType.DMA((steps,)),
            pltpu.SemaphoreType.DMA,
        ],
        compiler_params=params(40),
        cost_estimate=cost(4 * count * width * images, 4 * count * width),
    )(hid_a, hid_b, second, marks, classes, half)


def chunked(steps, tile, pairs, sem):
    def copies(i):
        rows = rows_at(i, tile)
        return [
            pltpu.make_async_copy(source.at[rows], target.at[rows], sem.at[p, i])
            for p, (source, target) in enumerate(pairs)
        ]

    def start(i):
        for copy in copies(i):
            copy.start()

    def wait(i):
        for copy in copies(i):
            copy.wait()

    return start, wait


def columns_of(classes):
    pad = jnp.zeros((-classes.shape[0] % 8, classes.shape[1]), jnp.int32)
    return jnp.concatenate([classes[...], pad]).T


def inverse_norm(block):
    return lax.rsqrt(jnp.sum(block * block, axis=1, keepdims=True) + NORM_EPSILON)


def terms_kernel(
    marks_hbm, classes_hbm, shared_hbm, out_hbm, marks, classes, half, unit, out, first_sem, in_sem, out_sem
):
    steps, tile = classes.shape
    count = steps * tile
    units = shared_hbm.at[pl.ds(count, unit.shape[0])]
    firsts = [
        pltpu.make_async_copy(source, place, first_sem.at[i])
        for i, (source, place) in enumerate(((marks_hbm, marks), (classes_hbm, classes), (units, unit)))
    ]
    for copy in firsts:
        copy.start()
    load, loaded = chunked(steps, tile, [(shared_hbm, half)], in_sem)
    store, stored = chunked(steps, tile, [(out, out_hbm)], out_sem)
    for i in range(min(AHEAD, steps)):
        load(i)
    for copy in firsts:
        copy.wait()
    columns = columns_of(classes)
    for i in range(steps):
        loaded(i)
        if i + AHEAD < steps:
            load(i + AHEAD)
        rows = rows_at(i, tile)
        cosine = dot(half[rows, :], unit[...], NT)
        positive = columns[:, i : i + 1] == marks[...]
        terms = exp_terms_of(cosine, positive)
        out[rows, :] = jnp.where(positive, -jnp.maximum(terms, SMALLEST), terms).astype(BF16)
        store(i)
    for i in range(steps):
        stored(i)


def turned_terms(classes, marks, shared):
    count, width = classes.size, shared.shape[1]
    images = marks.shape[1]
    steps = classes.shape[0]
    return pl.pallas_call(
        terms_kernel,
        in_specs=[HBM] * 3,
        out_specs=HBM,
        out_shape=jax.ShapeDtypeStruct((count, images), BF16),
        scratch_shapes=[
            pltpu.VMEM(marks.shape, jnp.int32),
            pltpu.VMEM(classes.shape, jnp.int32),
            pltpu.VMEM((count, width), BF16),
            pltpu.VMEM((images, width), BF16),
            pltpu.VMEM((count, images), BF16),
            pltpu.SemaphoreType.DMA((3,)),
            pltpu.SemaphoreType.DMA((1, steps)),
            pltpu.SemaphoreType.DMA((1, steps)),
        ],
        compiler_params=params(57),
        cost_estimate=cost(2 * count * width * images, 8 * count * width),
    )(marks, classes, shared)


def centres_kernel(
    factor,
    sent_hbm,
    cen_hbm,
    shared_hbm,
    terms_hbm,
    out_hbm,
    loss,
    sent,
    unit,
    cen,
    terms,
    out,
    first_sem,
    in_sem,
    out_sem,
):
    steps = in_sem.shape[1]
    count = cen.shape[0]
    tile = count // steps
    firsts = [
        pltpu.make_async_copy(sent_hbm, sent, first_sem.at[0]),
        pltpu.make_async_copy(shared_hbm.at[pl.ds(count, unit.shape[0])], unit, first_sem.at[1]),
    ]
    load, loaded = chunked(steps, tile, [(cen_hbm, cen), (terms_hbm, terms)], in_sem)
    store, stored = chunked(steps, tile, [(out, out_hbm)], out_sem)
    for copy in firsts:
        copy.start()
    for i in range(min(AHEAD + 1, steps)):
        load(i)
    for copy in firsts:
        copy.wait()
    width = unit.shape[1]
    riding = sent[:, width : width + unit.shape[0] // 2]
    halves = [riding[r : r + 1, :] + riding[r + 2 : r + 3, :] + riding[r + 4 : r + 5, :] for r in range(2)]
    totals = jnp.concatenate(halves, axis=1) * (1.0 / PIECE_SCALE)
    share = factor / totals
    for i in range(steps):
        loaded(i)
        if i + AHEAD + 1 < steps:
            load(i + AHEAD + 1)
        rows = rows_at(i, tile)
        block = cen[rows, :].astype(F32)
        inv = inverse_norm(block)
        signed = terms[rows, :].astype(F32)
        coeff = jnp.abs(signed) * share - jnp.where(signed < 0.0, factor, 0.0)
        grad = dot(coeff.astype(BF16), unit[...])
        along = jnp.sum(grad * block, axis=1, keepdims=True) * (inv * inv)
        out[rows, :] = (inv * (grad - block * along)).astype(BF16)
        store(i)
    loss[0, 0] = (jnp.sum(LOGIT_SCALE + jnp.log(totals)) - jnp.sum(riding[6:7, :])) / totals.shape[1]
    for i in range(steps):
        stored(i)


def grad_centres(centres, terms, shared, sent):
    count, width = centres.shape
    images = terms.shape[1]
    steps = count // tile_of(count, 640)
    return pl.pallas_call(
        functools.partial(centres_kernel, LOGIT_SCALE / images),
        in_specs=[HBM] * 4,
        out_specs=[HBM, pl.BlockSpec(memory_space=pltpu.SMEM)],
        out_shape=[
            jax.ShapeDtypeStruct((count, width), BF16),
            jax.ShapeDtypeStruct((1, 1), F32),
        ],
        scratch_shapes=[
            pltpu.VMEM(sent.shape, F32),
            pltpu.VMEM((images, width), BF16),
            pltpu.VMEM((count, width), BF16),
            pltpu.VMEM((count, images), BF16),
            pltpu.VMEM((count, width), BF16),
            pltpu.SemaphoreType.DMA((2,)),
            pltpu.SemaphoreType.DMA((2, steps)),
            pltpu.SemaphoreType.DMA((1, steps)),
        ],
        compiler_params=params(57),
        cost_estimate=cost(4 * count * width * images, 8 * count * width),
    )(sent, centres, shared, terms)


def turn_kernel(rows, place_ref, *refs):
    blocks, out_ref, stack = refs[:-2], refs[-2], refs[-1]
    group, depth = blocks[0].shape
    y = place_ref[0]
    for i, block in enumerate(blocks):
        dy, dc = divmod(i, 2)
        where = dc * rows + lax.rem(y - dy + rows, rows)
        stack[pl.ds(pl.multiple_of(where * group, group), group), :] = block[...]
    width = tile_of(depth, 128)

    if width == 128:

        def turn(i, carry):
            columns = pl.ds(pl.multiple_of(i * width, width), width)
            out_ref[columns, :] = stack[:, columns].T
            return carry

        lax.fori_loop(0, depth // width, turn, 0)
    else:
        out_ref[...] = stack[...].T


def turned(rows, place, blocks):
    group, depth = blocks[0].shape
    images = group * len(blocks)
    return pl.pallas_call(
        functools.partial(turn_kernel, rows),
        in_specs=[pl.BlockSpec(memory_space=pltpu.SMEM)] + [VMEM] * len(blocks),
        out_specs=VMEM,
        out_shape=jax.ShapeDtypeStruct((depth, images), BF16),
        scratch_shapes=[pltpu.VMEM((images, depth), BF16)],
        compiler_params=params(57),
        cost_estimate=cost(0, 4 * depth * images),
    )(place, *blocks)


def tail_kernel(
    grad_a,
    grad_b,
    hid_a,
    hid_b,
    second,
    features,
    first_hbm,
    second_out,
    out,
    grad_hidden,
    out_sem,
):
    group = grad_a.shape[0]
    steps = out_sem.shape[0]
    tile = out.shape[0] // steps

    def store(i):
        rows = rows_at(i, tile)
        return pltpu.make_async_copy(out.at[rows], first_hbm.at[rows], out_sem.at[i])

    acts = []
    for place, (grad, hid) in enumerate(((grad_a, hid_a), (grad_b, hid_b))):
        act, slope = gelu_parts(hid[...].astype(F32))
        acts.append(act.astype(BF16))
        grad_act = dot(grad[...], second[...], NT)
        grad_hidden[pl.ds(place * group, group), :] = (grad_act * slope).astype(BF16)

    def step(i):
        rows = rows_at(i, tile)
        out[rows, :] = dot(features[rows, :], grad_hidden[...]).astype(BF16)
        store(i).start()

    each(steps, True, step)
    act = jnp.concatenate(acts)
    grad = jnp.concatenate([grad_a[...], grad_b[...]])
    second_out[...] = dot(act.T, grad).astype(BF16)
    each(steps, True, lambda i: store(i).wait())


def tail(grad_a, grad_b, hid_a, hid_b, second, turned_features):
    depth, images = turned_features.shape
    hidden, width = second.shape
    steps = depth // tile_of(depth, 600)
    return pl.pallas_call(
        tail_kernel,
        in_specs=[VMEM] * 6,
        out_specs=[HBM, VMEM],
        out_shape=[
            jax.ShapeDtypeStruct((depth, hidden), BF16),
            jax.ShapeDtypeStruct((hidden, width), BF16),
        ],
        scratch_shapes=[
            pltpu.VMEM((depth, hidden), BF16),
            pltpu.VMEM((images, hidden), BF16),
            pltpu.SemaphoreType.DMA((steps,)),
        ],
        compiler_params=params(40),
        cost_estimate=cost(2 * depth * hidden * images, 2 * depth * (hidden + images)),
    )(grad_a, grad_b, hid_a, hid_b, second, turned_features)


def assemble_kernel(images, keep, got, picked, out):
    width = keep.shape[1]
    half = keep.shape[0] - 8
    each = -(-images // width)

    def sums(ref):
        lines = [
            jnp.concatenate([ref[half + each * q + r : half + each * q + r + 1, :] for r in range(each)], axis=1)
            for q in range(2)
        ]
        return jnp.concatenate(lines)[:, :images]

    other = sums(got)
    both = sums(keep) + jnp.concatenate([other[:, images // 2 :], other[:, : images // 2]], axis=1)
    total = both[0:1, :] * PIECE_SCALE
    target = jnp.broadcast_to(jnp.sum(both[1:2, :], axis=1, keepdims=True), (1, half))
    lane = lax.broadcasted_iota(jnp.int32, (1, half), 1)
    lines, last = [], jnp.zeros((1, half), F32)
    for i in range(3):
        part = total.astype(BF16).astype(F32)
        lines += [part[:, :half], part[:, half:]]
        total = total - part
        part = target.astype(BF16).astype(F32)
        last = jnp.where(lane == i, part, last)
        target = target - part
    riding = jnp.concatenate(lines + [last, jnp.zeros_like(last)])
    out[:, :width] = (keep[:half, :] + got[:half, :]).astype(BF16)
    out[:, width : width + half] = jnp.concatenate([riding] * (half // 8)).astype(BF16)
    out[:, width + half :] = picked[...]


def assemble(images, keep, got, picked):
    half, width = keep.shape[0] - 8, keep.shape[1]
    return pl.pallas_call(
        functools.partial(assemble_kernel, images),
        in_specs=[VMEM] * 3,
        out_specs=VMEM,
        out_shape=jax.ShapeDtypeStruct((half, width + half + picked.shape[1]), BF16),
        compiler_params=params(16),
        cost_estimate=cost(0, 8 * half * (width + images)),
    )(keep, got, picked)


def core_swap(x):
    return lax.ppermute(x, "core", [(0, 1), (1, 0)])


def to_chips(x):
    return lax.all_to_all(x, ("row", "gy"), 0, 0, tiled=True)


def to_all_chips(x, chips):
    x = to_chips(jnp.broadcast_to(x[None], (chips,) + x.shape))
    return x.reshape(-1, x.shape[-1])


def shards(features, first_weight, second_weight, centres, active, labels):
    rows, gy_count = lax.axis_size("row"), lax.axis_size("gy")
    y, core, gy = lax.axis_index("row"), lax.axis_index("core"), lax.axis_index("gy")
    chips = rows * gy_count
    chip = y * gy_count + gy
    device = (y * 2 + core) * gy_count + gy
    image_count = labels.shape[0]
    half = image_count // 2
    group = features.shape[0]
    own = half // chips
    depth = first_weight.shape[0]

    blocks = {}
    others = list(range(1, rows))
    for dy, dc in [(dy, 1) for dy in others] + [(0, 1)] + [(dy, 0) for dy in others] + [(0, 0)]:
        target = ((y + dy) % rows) * 2 + (core ^ dc)
        if (dy, dc) == (0, 0):
            source, labels = lax.optimization_barrier((features, labels))
            blocks[dy, dc] = lax.dynamic_slice_in_dim(source, target * depth, depth, axis=1)
            continue
        part = lax.dynamic_slice_in_dim(features, target * depth, depth, axis=1)
        perm = [
            (a * 2 + b, ((a + dy) % rows) * 2 + (b ^ dc)) for a in range(rows) for b in range(2)
        ]
        blocks[dy, dc] = lax.ppermute(part, ("row", "core"), perm)

    marks = labels.reshape(rows, 2, group).transpose(1, 0, 2)
    marks = jnp.where(core == 0, marks, marks[::-1]).reshape(image_count)
    marks = marks[None, :]
    count = active.shape[0]
    tile = tile_of(count, 1280 if image_count <= 256 else 256)
    classes = (device * CLS_DEV + active).reshape(count // tile, tile)

    first_arrived, marks, classes = lax.optimization_barrier((blocks[0, 1], marks, classes))
    blocks[0, 1] = first_arrived
    normed_half, picked = prep(centres, marks, classes)
    picked = picked[:half] + core_swap(picked[half:])

    def partial_hidden(*names):
        return jnp.dot(
            jnp.concatenate([blocks[n] for n in names]), first_weight, preferred_element_type=F32
        )

    near = partial_hidden((0, 1), (0, 0))
    early = [blocks[dy, 1] for dy in others]
    early, near, normed_half, picked = lax.optimization_barrier((early, near, normed_half, picked))
    for dy, block in zip(others, early):
        blocks[dy, 1] = block
    far_send = partial_hidden(*[(dy, 1) for dy in others])
    near_keep = near[group:] + core_swap(near[:group])
    far_got = core_swap(far_send)
    last = [blocks[dy, 0] for dy in others]
    last, far_got, near_keep, picked = lax.optimization_barrier((last, far_got, near_keep, picked))
    for dy, block in zip(others, last):
        blocks[dy, 0] = block
    far_keep = partial_hidden(*[(dy, 0) for dy in others]) + far_got
    if rows == 2:
        part = jnp.where(
            y == 0,
            jnp.concatenate([near_keep, far_keep]),
            jnp.concatenate([far_keep, near_keep]),
        )
    else:
        part = jnp.concatenate([near_keep, far_keep]).reshape(rows, group, -1)
        part = part[(y - jnp.arange(rows)) % rows].reshape(half, -1)
    wide = part.shape[1]
    part = part.astype(BF16)
    part = to_chips(part.reshape(chips, own, -1))
    place = jnp.reshape(y, (1,)).astype(jnp.int32)
    order = [(dy, dc) for dy in range(rows) for dc in range(2)]
    turned_features = turned(rows, place, [blocks[n] for n in order])
    part, turned_features = lax.optimization_barrier((part, turned_features))
    part = jnp.sum(part.astype(F32), axis=0)
    hidden_own = part.astype(BF16)
    hid_a = to_all_chips(hidden_own, chips)
    hid_b = core_swap(hid_a)

    embed_own = jnp.dot(
        gelu_parts(hidden_own.astype(F32))[0].astype(BF16), second_weight, preferred_element_type=F32
    )
    inv_own = lax.rsqrt(jnp.sum(embed_own * embed_own, axis=1, keepdims=True) + NORM_EPSILON)
    unit_own = embed_own * inv_own

    weighted, weighted_send, shared = softmax_sums(
        hid_a, hid_b, second_weight, marks, classes, normed_half
    )
    width = weighted.shape[1]
    sent = assemble(image_count, weighted, core_swap(weighted_send), picked)
    sent, shared = lax.optimization_barrier((sent, shared))
    terms = turned_terms(classes, marks, shared)
    sent, terms = lax.optimization_barrier((to_chips(sent.reshape(chips, own, -1)), terms))
    sent = jnp.sum(sent.astype(F32), axis=0)
    weighted, riding = sent[:, :width], sent[:, width : width + half]
    picked = sent[:, width + half :]
    totals = riding[:6].reshape(3, image_count).sum(axis=0, keepdims=True)
    totals = totals * (1.0 / PIECE_SCALE)

    factor = LOGIT_SCALE / image_count
    totals_own = lax.dynamic_slice_in_dim(totals, chip * own, own, axis=1).reshape(own, 1)
    grad_unit = factor * (weighted / totals_own - picked)
    grad_embed = inv_own * (grad_unit - unit_own * jnp.sum(grad_unit * unit_own, axis=1, keepdims=True))
    grad_embed = grad_embed.astype(BF16)
    grad_embed = jnp.broadcast_to(grad_embed[None], (chips,) + grad_embed.shape)
    grad_cen, loss = grad_centres(centres, terms, shared, sent)
    grad_a = to_chips(grad_embed).reshape(half, -1)
    grad_a, grad_cen, turned_features = lax.optimization_barrier((grad_a, grad_cen, turned_features))
    grad_b = core_swap(grad_a)
    grad_first, grad_second = tail(grad_a, grad_b, hid_a, hid_b, second_weight, turned_features)
    return loss.reshape(()), grad_first, grad_second, grad_cen


def solution(mesh):
    gx_count, gy_count = mesh.shape["gx"], mesh.shape["gy"]
    fine = Mesh(mesh.devices.reshape(gx_count // 2, 2, gy_count), ("row", "core", "gy"))
    gx = ("row", "core")
    placed = (
        P(gx, "gy"),
        P(("gy",) + gx, None),
        P(),
        P(gx + ("gy",), None),
        P(gx + ("gy",)),
        P(),
    )
    return jax.shard_map(
        shards,
        mesh=fine,
        in_specs=placed,
        out_specs=(P(), P(("gy",) + gx, None), P(), P(gx + ("gy",), None)),
        check_vma=False,
    )
```

```python
import functools

import jax
import jax.numpy as jnp
from jax import lax
from jax.experimental import pallas as pl
from jax.experimental.pallas import tpu as pltpu
from jax.sharding import Mesh, PartitionSpec as P

CLS_DEV = 16128


LOGIT_SCALE = 64.0
COS_MARGIN = 0.4
NORM_EPSILON = 1e-06

POWER = LOGIT_SCALE * 1.4426950408889634

PIECE_SCALE = 2.0**64

SMALLEST = 1.1754944e-38

AHEAD = 2

F32, BF16 = jnp.float32, jnp.bfloat16
MIB = 2**20
VMEM = pl.BlockSpec(memory_space=pltpu.VMEM)
HBM = pl.BlockSpec(memory_space=pltpu.HBM)

NN = (((1,), (0,)), ((), ()))
NT = (((1,), (1,)), ((), ()))


def dot(a, b, dims=NN):
    return lax.dot_general(a, b, dims, preferred_element_type=F32)


def tile_of(extent, most, unit=16):
    return max(t for t in range(unit, most + 1, unit) if extent % t == 0)


def gelu_parts(v):
    scale = 0.7978845608028654
    cube = 0.044715
    square = v * v
    bend = jnp.tanh(scale * (v + cube * square * v))
    left = 0.5 * (1.0 + bend)
    slope = left + 0.5 * v * (1.0 - bend * bend) * scale * (1.0 + 3.0 * cube * square)
    return v * left, slope


def row_to_column(row):
    return jnp.broadcast_to(row, (8, row.shape[1])).T[:, :1]


def each(count, plain, step):
    if plain:
        for i in range(count):
            step(i)
    else:

        def run(i, carry):
            step(i)
            return carry

        lax.fori_loop(0, count, run, 0)


def rows_at(i, tile):
    return pl.ds(i * tile if isinstance(i, int) else pl.multiple_of(i * tile, tile), tile)


def params(mib):
    return pltpu.CompilerParams(vmem_limit_bytes=mib * MIB)


def cost(flops, moved):
    return pl.CostEstimate(flops=flops, bytes_accessed=moved, transcendentals=0)


def exp_terms_of(cosine, positive):
    return jnp.exp2(
        cosine * POWER - jnp.where(positive, POWER * (1.0 + COS_MARGIN), POWER)
    )


def prep_kernel(plain, marks, classes, cen_hbm, half_hbm, picked, cen, half, total, in_sem, out_sem):
    steps, tile = classes.shape
    column = row_to_column(marks[...])

    def load(i):
        rows = rows_at(i, tile)
        return pltpu.make_async_copy(cen_hbm.at[rows], cen.at[rows], in_sem.at[i])

    def store(i):
        rows = rows_at(i, tile)
        return pltpu.make_async_copy(half.at[rows], half_hbm.at[rows], out_sem.at[i])

    each(steps, plain, lambda i: load(i).start())
    total[...] = jnp.zeros_like(total)

    def step(i):
        load(i).wait()
        rows = rows_at(i, tile)
        block = cen[rows, :].astype(F32)
        inv = lax.rsqrt(jnp.sum(block * block, axis=1, keepdims=True) + NORM_EPSILON)
        block = (block * inv).astype(BF16)
        half[rows, :] = block
        store(i).start()
        match = jnp.where(column == classes[pl.ds(i, 1), :], 1.0, 0.0).astype(BF16)
        total[...] += dot(match, block)

    each(steps, plain, step)
    picked[...] = total[...].astype(BF16)
    each(steps, plain, lambda i: store(i).wait())


def prep(centres, marks, classes):
    count, width = centres.shape
    images = marks.shape[1]
    steps = classes.shape[0]
    return pl.pallas_call(
        functools.partial(prep_kernel, images <= 256),
        in_specs=[VMEM, VMEM, HBM],
        out_specs=[HBM, VMEM],
        out_shape=[
            jax.ShapeDtypeStruct((5 * count, width), BF16),
            jax.ShapeDtypeStruct((images, width), BF16),
        ],
        scratch_shapes=[
            pltpu.VMEM((count, width), BF16),
            pltpu.VMEM((count, width), BF16),
            pltpu.VMEM((images, width), F32),
            pltpu.SemaphoreType.DMA((steps,)),
            pltpu.SemaphoreType.DMA((steps,)),
        ],
        compiler_params=params(28),
        cost_estimate=cost(2 * count * width * images, 8 * count * width),
    )(marks, classes, centres)


def softmax_kernel(
    plain,
    hid_a_hbm,
    hid_b_hbm,
    second_hbm,
    marks,
    classes,
    half_hbm,
    keep,
    send,
    shared,
    hid_a,
    hid_b,
    second,
    half,
    unit,
    weighted,
    first_sem,
    in_sem,
    out_sem,
):
    steps, tile = classes.shape
    firsts = [
        pltpu.make_async_copy(source, place, first_sem.at[i])
        for i, (source, place) in enumerate(
            ((hid_a_hbm, hid_a), (second_hbm, second), (hid_b_hbm, hid_b))
        )
    ]
    for copy in firsts:
        copy.start()

    def load(i):
        rows = rows_at(i, tile)
        return pltpu.make_async_copy(half_hbm.at[rows], half.at[rows], in_sem.at[i])

    load(0).start()
    group = hid_a.shape[0]
    images = 2 * group
    column = row_to_column(marks[...])
    firsts[0].wait()
    firsts[1].wait()
    each(steps - 1, plain, lambda i: load(i + 1).start())
    for place, hid in enumerate((hid_a, hid_b)):
        if place == 1:
            firsts[2].wait()
        act, _ = gelu_parts(hid[...].astype(F32))
        embedding = dot(act.astype(BF16), second[...])
        inv = lax.rsqrt(jnp.sum(embedding * embedding, axis=1, keepdims=True) + NORM_EPSILON)
        unit[pl.ds(place * group, group), :] = (embedding * inv).astype(BF16)
    store = pltpu.make_async_copy(unit, shared.at[pl.ds(steps * tile, images)], out_sem)
    store.start()
    weighted[...] = jnp.zeros_like(weighted)

    def step(i, sums):
        load(i).wait()
        block = half[rows_at(i, tile), :]
        cosine = dot(unit[...], block, NT)
        positive = column == classes[pl.ds(i, 1), :]
        exp_terms = exp_terms_of(cosine, positive)
        weighted[...] += dot(exp_terms.astype(BF16), block)
        total = jnp.sum(exp_terms, axis=1, keepdims=True)
        target = jnp.sum(jnp.where(positive, cosine - COS_MARGIN, 0.0), axis=1, keepdims=True)
        return sums[0] + total, sums[1] + target

    total = target = jnp.zeros((images, 1), F32)
    if plain:
        for i in range(steps):
            total, target = step(i, (total, target))
    else:
        total, target = lax.fori_loop(0, steps, step, (total, target))
    sums = [jnp.broadcast_to(x, (images, 128)).T[:1] for x in (total * PIECE_SCALE, LOGIT_SCALE * target)]
    width = keep.shape[1]
    rows = [x[:, c : c + width] for x in sums for c in range(0, images, width)]
    rows = [jnp.pad(x, ((0, 0), (0, width - x.shape[1]))) for x in rows]
    rows = jnp.concatenate(rows + [jnp.zeros((8 - len(rows), width), F32)])
    keep[:group, :] = weighted[:group]
    keep[group:, :] = rows
    send[:group, :] = weighted[group:].astype(BF16)
    cut = []
    for _ in range(3):
        part = rows.astype(BF16).astype(F32)
        cut.append(part)
        rows = rows - part
    send[group:, :] = jnp.concatenate(cut + [jnp.zeros_like(rows)]).astype(BF16)
    store.wait()


def softmax_sums(hid_a, hid_b, second, marks, classes, half):
    width = half.shape[1]
    group = hid_a.shape[0]
    images = marks.shape[1]
    steps = classes.shape[0]
    count = classes.size
    return pl.pallas_call(
        functools.partial(softmax_kernel, images <= 256),
        in_specs=[HBM] * 3 + [VMEM] * 2 + [HBM],
        out_specs=[VMEM] * 2 + [HBM],
        input_output_aliases={5: 2},
        out_shape=[
            jax.ShapeDtypeStruct((group + 8, width), F32),
            jax.ShapeDtypeStruct((group + 32, width), BF16),
            jax.ShapeDtypeStruct(half.shape, BF16),
        ],
        scratch_shapes=[
            pltpu.VMEM(hid_a.shape, BF16),
            pltpu.VMEM(hid_b.shape, BF16),
            pltpu.VMEM(second.shape, BF16),
            pltpu.VMEM((count, width), BF16),
            pltpu.VMEM((images, width), BF16),
            pltpu.VMEM((images, width), F32),
            pltpu.SemaphoreType.DMA((3,)),
            pltpu.SemaphoreType.DMA((steps,)),
            pltpu.SemaphoreType.DMA,
        ],
        compiler_params=params(40),
        cost_estimate=cost(4 * count * width * images, 4 * count * width),
    )(hid_a, hid_b, second, marks, classes, half)


def chunked(steps, tile, pairs, sem):
    def copies(i):
        rows = rows_at(i, tile)
        return [
            pltpu.make_async_copy(source.at[rows], target.at[rows], sem.at[p, i])
            for p, (source, target) in enumerate(pairs)
        ]

    def start(i):
        for copy in copies(i):
            copy.start()

    def wait(i):
        for copy in copies(i):
            copy.wait()

    return start, wait


def columns_of(classes):
    pad = jnp.zeros((-classes.shape[0] % 8, classes.shape[1]), jnp.int32)
    return jnp.concatenate([classes[...], pad]).T


def inverse_norm(block):
    return lax.rsqrt(jnp.sum(block * block, axis=1, keepdims=True) + NORM_EPSILON)


def terms_kernel(
    marks_hbm, classes_hbm, shared_hbm, out_hbm, marks, classes, half, unit, out, first_sem, in_sem, out_sem
):
    steps, tile = classes.shape
    count = steps * tile
    units = shared_hbm.at[pl.ds(count, unit.shape[0])]
    firsts = [
        pltpu.make_async_copy(source, place, first_sem.at[i])
        for i, (source, place) in enumerate(((marks_hbm, marks), (classes_hbm, classes), (units, unit)))
    ]
    for copy in firsts:
        copy.start()
    load, loaded = chunked(steps, tile, [(shared_hbm, half)], in_sem)
    store, stored = chunked(steps, tile, [(out, out_hbm)], out_sem)
    for i in range(min(AHEAD, steps)):
        load(i)
    for copy in firsts:
        copy.wait()
    columns = columns_of(classes)
    for i in range(steps):
        loaded(i)
        if i + AHEAD < steps:
            load(i + AHEAD)
        rows = rows_at(i, tile)
        cosine = dot(half[rows, :], unit[...], NT)
        positive = columns[:, i : i + 1] == marks[...]
        terms = exp_terms_of(cosine, positive)
        out[rows, :] = jnp.where(positive, -jnp.maximum(terms, SMALLEST), terms).astype(BF16)
        store(i)
    for i in range(steps):
        stored(i)


def turned_terms(classes, marks, shared):
    count, width = classes.size, shared.shape[1]
    images = marks.shape[1]
    steps = classes.shape[0]
    return pl.pallas_call(
        terms_kernel,
        in_specs=[HBM] * 3,
        out_specs=HBM,
        out_shape=jax.ShapeDtypeStruct((count, images), BF16),
        scratch_shapes=[
            pltpu.VMEM(marks.shape, jnp.int32),
            pltpu.VMEM(classes.shape, jnp.int32),
            pltpu.VMEM((count, width), BF16),
            pltpu.VMEM((images, width), BF16),
            pltpu.VMEM((count, images), BF16),
            pltpu.SemaphoreType.DMA((3,)),
            pltpu.SemaphoreType.DMA((1, steps)),
            pltpu.SemaphoreType.DMA((1, steps)),
        ],
        compiler_params=params(57),
        cost_estimate=cost(2 * count * width * images, 8 * count * width),
    )(marks, classes, shared)


def centres_kernel(
    factor,
    sent_hbm,
    cen_hbm,
    shared_hbm,
    terms_hbm,
    out_hbm,
    loss,
    sent,
    unit,
    cen,
    terms,
    out,
    first_sem,
    in_sem,
    out_sem,
):
    steps = in_sem.shape[1]
    count = cen.shape[0]
    tile = count // steps
    firsts = [
        pltpu.make_async_copy(sent_hbm, sent, first_sem.at[0]),
        pltpu.make_async_copy(shared_hbm.at[pl.ds(count, unit.shape[0])], unit, first_sem.at[1]),
    ]
    load, loaded = chunked(steps, tile, [(cen_hbm, cen), (terms_hbm, terms)], in_sem)
    store, stored = chunked(steps, tile, [(out, out_hbm)], out_sem)
    for copy in firsts:
        copy.start()
    for i in range(min(AHEAD + 1, steps)):
        load(i)
    for copy in firsts:
        copy.wait()
    width = unit.shape[1]
    riding = sent[:, width : width + unit.shape[0] // 2]
    halves = [riding[r : r + 1, :] + riding[r + 2 : r + 3, :] + riding[r + 4 : r + 5, :] for r in range(2)]
    totals = jnp.concatenate(halves, axis=1) * (1.0 / PIECE_SCALE)
    share = factor / totals
    for i in range(steps):
        loaded(i)
        if i + AHEAD + 1 < steps:
            load(i + AHEAD + 1)
        rows = rows_at(i, tile)
        block = cen[rows, :].astype(F32)
        inv = inverse_norm(block)
        signed = terms[rows, :].astype(F32)
        coeff = jnp.abs(signed) * share - jnp.where(signed < 0.0, factor, 0.0)
        grad = dot(coeff.astype(BF16), unit[...])
        along = jnp.sum(grad * block, axis=1, keepdims=True) * (inv * inv)
        out[rows, :] = (inv * (grad - block * along)).astype(BF16)
        store(i)
    loss[0, 0] = (jnp.sum(LOGIT_SCALE + jnp.log(totals)) - jnp.sum(riding[6:7, :])) / totals.shape[1]
    for i in range(steps):
        stored(i)


def grad_centres(centres, terms, shared, sent):
    count, width = centres.shape
    images = terms.shape[1]
    steps = count // tile_of(count, 640)
    return pl.pallas_call(
        functools.partial(centres_kernel, LOGIT_SCALE / images),
        in_specs=[HBM] * 4,
        out_specs=[HBM, pl.BlockSpec(memory_space=pltpu.SMEM)],
        out_shape=[
            jax.ShapeDtypeStruct((count, width), BF16),
            jax.ShapeDtypeStruct((1, 1), F32),
        ],
        scratch_shapes=[
            pltpu.VMEM(sent.shape, F32),
            pltpu.VMEM((images, width), BF16),
            pltpu.VMEM((count, width), BF16),
            pltpu.VMEM((count, images), BF16),
            pltpu.VMEM((count, width), BF16),
            pltpu.SemaphoreType.DMA((2,)),
            pltpu.SemaphoreType.DMA((2, steps)),
            pltpu.SemaphoreType.DMA((1, steps)),
        ],
        compiler_params=params(57),
        cost_estimate=cost(4 * count * width * images, 8 * count * width),
    )(sent, centres, shared, terms)


def turn_kernel(rows, place_ref, *refs):
    blocks, out_ref, stack = refs[:-2], refs[-2], refs[-1]
    group, depth = blocks[0].shape
    y = place_ref[0]
    for i, block in enumerate(blocks):
        dy, dc = divmod(i, 2)
        where = dc * rows + lax.rem(y - dy + rows, rows)
        stack[pl.ds(pl.multiple_of(where * group, group), group), :] = block[...]
    width = tile_of(depth, 128)

    if width == 128:

        def turn(i, carry):
            columns = pl.ds(pl.multiple_of(i * width, width), width)
            out_ref[columns, :] = stack[:, columns].T
            return carry

        lax.fori_loop(0, depth // width, turn, 0)
    else:
        out_ref[...] = stack[...].T


def turned(rows, place, blocks):
    group, depth = blocks[0].shape
    images = group * len(blocks)
    return pl.pallas_call(
        functools.partial(turn_kernel, rows),
        in_specs=[pl.BlockSpec(memory_space=pltpu.SMEM)] + [VMEM] * len(blocks),
        out_specs=VMEM,
        out_shape=jax.ShapeDtypeStruct((depth, images), BF16),
        scratch_shapes=[pltpu.VMEM((images, depth), BF16)],
        compiler_params=params(57),
        cost_estimate=cost(0, 4 * depth * images),
    )(place, *blocks)


def tail_kernel(
    grad_a,
    grad_b,
    hid_a,
    hid_b,
    second,
    features,
    first_hbm,
    second_out,
    out,
    grad_hidden,
    out_sem,
):
    group = grad_a.shape[0]
    steps = out_sem.shape[0]
    tile = out.shape[0] // steps

    def store(i):
        rows = rows_at(i, tile)
        return pltpu.make_async_copy(out.at[rows], first_hbm.at[rows], out_sem.at[i])

    acts = []
    for place, (grad, hid) in enumerate(((grad_a, hid_a), (grad_b, hid_b))):
        act, slope = gelu_parts(hid[...].astype(F32))
        acts.append(act.astype(BF16))
        grad_act = dot(grad[...], second[...], NT)
        grad_hidden[pl.ds(place * group, group), :] = (grad_act * slope).astype(BF16)

    def step(i):
        rows = rows_at(i, tile)
        out[rows, :] = dot(features[rows, :], grad_hidden[...]).astype(BF16)
        store(i).start()

    each(steps, True, step)
    act = jnp.concatenate(acts)
    grad = jnp.concatenate([grad_a[...], grad_b[...]])
    second_out[...] = dot(act.T, grad).astype(BF16)
    each(steps, True, lambda i: store(i).wait())


def tail(grad_a, grad_b, hid_a, hid_b, second, turned_features):
    depth, images = turned_features.shape
    hidden, width = second.shape
    steps = depth // tile_of(depth, 600)
    return pl.pallas_call(
        tail_kernel,
        in_specs=[VMEM] * 6,
        out_specs=[HBM, VMEM],
        out_shape=[
            jax.ShapeDtypeStruct((depth, hidden), BF16),
            jax.ShapeDtypeStruct((hidden, width), BF16),
        ],
        scratch_shapes=[
            pltpu.VMEM((depth, hidden), BF16),
            pltpu.VMEM((images, hidden), BF16),
            pltpu.SemaphoreType.DMA((steps,)),
        ],
        compiler_params=params(40),
        cost_estimate=cost(2 * depth * hidden * images, 2 * depth * (hidden + images)),
    )(grad_a, grad_b, hid_a, hid_b, second, turned_features)


def assemble_kernel(images, keep, got, picked, out):
    width = keep.shape[1]
    half = keep.shape[0] - 8
    each = -(-images // width)

    def sums(rows):
        lines = [
            jnp.concatenate([rows[each * q + r : each * q + r + 1, :] for r in range(each)], axis=1)
            for q in range(2)
        ]
        return jnp.concatenate(lines)[:, :images]

    cut = got[half:, :].astype(F32)
    other = sums(cut[:8] + cut[8:16] + cut[16:24])
    both = sums(keep[half:, :]) + jnp.concatenate([other[:, images // 2 :], other[:, : images // 2]], axis=1)
    total = both[0:1, :]
    target = jnp.broadcast_to(jnp.sum(both[1:2, :], axis=1, keepdims=True), (1, half))
    lane = lax.broadcasted_iota(jnp.int32, (1, half), 1)
    lines, last = [], jnp.zeros((1, half), F32)
    for i in range(3):
        part = total.astype(BF16).astype(F32)
        lines += [part[:, :half], part[:, half:]]
        total = total - part
        part = target.astype(BF16).astype(F32)
        last = jnp.where(lane == i, part, last)
        target = target - part
    riding = jnp.concatenate(lines + [last, jnp.zeros_like(last)])
    out[:, :width] = (keep[:half, :] + got[:half, :].astype(F32)).astype(BF16)
    out[:, width : width + half] = jnp.concatenate([riding] * (half // 8)).astype(BF16)
    out[:, width + half :] = picked[...]


def assemble(images, keep, got, picked):
    half, width = keep.shape[0] - 8, keep.shape[1]
    return pl.pallas_call(
        functools.partial(assemble_kernel, images),
        in_specs=[VMEM] * 3,
        out_specs=VMEM,
        out_shape=jax.ShapeDtypeStruct((half, width + half + picked.shape[1]), BF16),
        compiler_params=params(16),
        cost_estimate=cost(0, 8 * half * (width + images)),
    )(keep, got, picked)


def core_swap(x):
    return lax.ppermute(x, "core", [(0, 1), (1, 0)])


def to_chips(x):
    return lax.all_to_all(x, ("row", "gy"), 0, 0, tiled=True)


def to_all_chips(x, chips):
    x = to_chips(jnp.broadcast_to(x[None], (chips,) + x.shape))
    return x.reshape(-1, x.shape[-1])


def shards(features, first_weight, second_weight, centres, active, labels):
    rows, gy_count = lax.axis_size("row"), lax.axis_size("gy")
    y, core, gy = lax.axis_index("row"), lax.axis_index("core"), lax.axis_index("gy")
    chips = rows * gy_count
    chip = y * gy_count + gy
    device = (y * 2 + core) * gy_count + gy
    image_count = labels.shape[0]
    half = image_count // 2
    group = features.shape[0]
    own = half // chips
    depth = first_weight.shape[0]

    blocks = {}
    others = list(range(1, rows))
    for dy, dc in [(dy, 1) for dy in others] + [(0, 1)] + [(dy, 0) for dy in others] + [(0, 0)]:
        target = ((y + dy) % rows) * 2 + (core ^ dc)
        if (dy, dc) == (0, 0):
            source, labels = lax.optimization_barrier((features, labels))
            blocks[dy, dc] = lax.dynamic_slice_in_dim(source, target * depth, depth, axis=1)
            continue
        part = lax.dynamic_slice_in_dim(features, target * depth, depth, axis=1)
        perm = [
            (a * 2 + b, ((a + dy) % rows) * 2 + (b ^ dc)) for a in range(rows) for b in range(2)
        ]
        blocks[dy, dc] = lax.ppermute(part, ("row", "core"), perm)

    marks = labels.reshape(rows, 2, group).transpose(1, 0, 2)
    marks = jnp.where(core == 0, marks, marks[::-1]).reshape(image_count)
    marks = marks[None, :]
    count = active.shape[0]
    tile = tile_of(count, 1280 if image_count <= 256 else 256)
    classes = (device * CLS_DEV + active).reshape(count // tile, tile)

    first_arrived, marks, classes = lax.optimization_barrier((blocks[0, 1], marks, classes))
    blocks[0, 1] = first_arrived
    normed_half, picked = prep(centres, marks, classes)
    picked = picked[:half] + core_swap(picked[half:])

    def partial_hidden(*names):
        return jnp.dot(
            jnp.concatenate([blocks[n] for n in names]), first_weight, preferred_element_type=F32
        )

    near = partial_hidden((0, 1), (0, 0))
    early = [blocks[dy, 1] for dy in others]
    early, near, normed_half, picked = lax.optimization_barrier((early, near, normed_half, picked))
    for dy, block in zip(others, early):
        blocks[dy, 1] = block
    far_send = partial_hidden(*[(dy, 1) for dy in others])
    near_keep = near[group:] + core_swap(near[:group])
    far_got = core_swap(far_send)
    last = [blocks[dy, 0] for dy in others]
    last, far_got, near_keep, picked = lax.optimization_barrier((last, far_got, near_keep, picked))
    for dy, block in zip(others, last):
        blocks[dy, 0] = block
    far_keep = partial_hidden(*[(dy, 0) for dy in others]) + far_got
    if rows == 2:
        part = jnp.where(
            y == 0,
            jnp.concatenate([near_keep, far_keep]),
            jnp.concatenate([far_keep, near_keep]),
        )
    else:
        part = jnp.concatenate([near_keep, far_keep]).reshape(rows, group, -1)
        part = part[(y - jnp.arange(rows)) % rows].reshape(half, -1)
    wide = part.shape[1]
    part = part.astype(BF16)
    part = to_chips(part.reshape(chips, own, -1))
    place = jnp.reshape(y, (1,)).astype(jnp.int32)
    order = [(dy, dc) for dy in range(rows) for dc in range(2)]
    turned_features = turned(rows, place, [blocks[n] for n in order])
    part, turned_features = lax.optimization_barrier((part, turned_features))
    part = jnp.sum(part.astype(F32), axis=0)
    hidden_own = part.astype(BF16)
    hid_a = to_all_chips(hidden_own, chips)
    hid_b = core_swap(hid_a)

    embed_own = jnp.dot(
        gelu_parts(hidden_own.astype(F32))[0].astype(BF16), second_weight, preferred_element_type=F32
    )
    inv_own = lax.rsqrt(jnp.sum(embed_own * embed_own, axis=1, keepdims=True) + NORM_EPSILON)
    unit_own = embed_own * inv_own

    weighted, weighted_send, shared = softmax_sums(
        hid_a, hid_b, second_weight, marks, classes, normed_half
    )
    width = weighted.shape[1]
    sent = assemble(image_count, weighted, core_swap(weighted_send), picked)
    sent, shared = lax.optimization_barrier((sent, shared))
    terms = turned_terms(classes, marks, shared)
    sent, terms = lax.optimization_barrier((to_chips(sent.reshape(chips, own, -1)), terms))
    sent = jnp.sum(sent.astype(F32), axis=0)
    weighted, riding = sent[:, :width], sent[:, width : width + half]
    picked = sent[:, width + half :]
    totals = riding[:6].reshape(3, image_count).sum(axis=0, keepdims=True)
    totals = totals * (1.0 / PIECE_SCALE)

    factor = LOGIT_SCALE / image_count
    totals_own = lax.dynamic_slice_in_dim(totals, chip * own, own, axis=1).reshape(own, 1)
    grad_unit = factor * (weighted / totals_own - picked)
    grad_embed = inv_own * (grad_unit - unit_own * jnp.sum(grad_unit * unit_own, axis=1, keepdims=True))
    grad_embed = grad_embed.astype(BF16)
    grad_embed = jnp.broadcast_to(grad_embed[None], (chips,) + grad_embed.shape)
    grad_cen, loss = grad_centres(centres, terms, shared, sent)
    grad_a = to_chips(grad_embed).reshape(half, -1)
    grad_a, grad_cen, turned_features = lax.optimization_barrier((grad_a, grad_cen, turned_features))
    grad_b = core_swap(grad_a)
    grad_first, grad_second = tail(grad_a, grad_b, hid_a, hid_b, second_weight, turned_features)
    return loss.reshape(()), grad_first, grad_second, grad_cen


def solution(mesh):
    gx_count, gy_count = mesh.shape["gx"], mesh.shape["gy"]
    fine = Mesh(mesh.devices.reshape(gx_count // 2, 2, gy_count), ("row", "core", "gy"))
    gx = ("row", "core")
    placed = (
        P(gx, "gy"),
        P(("gy",) + gx, None),
        P(),
        P(gx + ("gy",), None),
        P(gx + ("gy",)),
        P(),
    )
    return jax.shard_map(
        shards,
        mesh=fine,
        in_specs=placed,
        out_specs=(P(), P(("gy",) + gx, None), P(), P(gx + ("gy",), None)),
        check_vma=False,
    )
```
